128 devices in a mesh: lat: 32 (over y, z, core), dep: 4 (over x).
Axes of the slice: x: 4, y: 4, z: 4, core: 2. Of those that a mesh axis runs over, the one named last changes fastest.
Arguments:
- stored_energy_density: float32 [128, 32, 4096], P('dep', None, 'lat'), may hold values from 0.2 to 3
- zones: int32 [32, 4096], P(None, 'lat'), may hold values from 0 to 15
- fluence: float32 [16], replicated, may hold values from 5 to 40
- seed_adjoint: float32 [128, 32, 4096], P('dep', None, 'lat'), may hold values from -6 to 6
Outputs:
- adjoint_start: float32 [128, 32, 4096], P('dep', None, 'lat')
- fluence_grad: float32 [16], replicated
The draws below stay inside these ranges and needn't reach their ends.
All inputs are finite; a program needn't handle non-finite values.
Results may differ from the reference program's by a relative error of at most 0.00021.
Values sent between devices are 32-bit elements; how exact they have to be, the bound alone decides.
No kernel may reach another device: no remote copies, remote signals or barrier semaphores. Data moves between devices by JAX's collectives and lax.ppermute only.
A program may use at most 128 MiB of HBM per device.

```python
import math
from functools import partial
import jax
import jax.numpy as jnp
from jax import lax

ROWS = 32
NZ = 128
STEPS = 4
NZONE = 16
NC = 4096


def place_ends(array, rng, low, top_value):
    index_at = [jax.random.randint(jax.random.fold_in(rng, axis), (), 0, length) for axis, length in enumerate(array.shape)]
    main_axis = array.shape.index(max(array.shape))
    next_to = index_at[:main_axis] + [(index_at[main_axis] + 1) % array.shape[main_axis]] + index_at[main_axis + 1:]
    return array.at[tuple(index_at)].set(low).at[tuple(next_to)].set(top_value)


def level_of(rng, dims, cuts, smallest, largest):
    factor_of, own = 1.0, jax.random.fold_in(rng, 6)
    for axis_at, blocks in cuts:
        steps = jnp.exp(jax.random.uniform(jax.random.fold_in(own, axis_at), (blocks,), jnp.float32, smallest / len(cuts), largest / len(cuts)))
        factor_of = factor_of * jnp.repeat(steps, dims[axis_at] // blocks).reshape([-1 if axis == axis_at else 1 for axis in range(len(dims))])
    return factor_of


def gaussian(own_key, extent, scale, bound, cuts=(), kind=jnp.bfloat16):
    gain = level_of(own_key, extent, cuts, -0.22, 0.18) if cuts else 1.0
    result = jax.random.normal(own_key, extent, jnp.float32) * scale * gain
    return jnp.minimum(jnp.maximum(result, -bound), bound).astype(kind)


def setup_inputs(seed: int = 0) -> dict:
    arg_keys = jax.random.split(jax.random.key(seed), 5)
    stored_energy_density = jnp.clip(0.2 + 2.8 * jax.random.uniform(arg_keys[0], (NZ, ROWS, NC), jnp.float32) ** level_of(arg_keys[0], (NZ, ROWS, NC), ((0, 4), (2, 32)), -0.2, 0.2), 0.2, 3.0)
    zones = place_ends(jax.random.randint(arg_keys[1], (ROWS, NC), 0, NZONE), jax.random.fold_in(arg_keys[1], 1), 0, NZONE - 1).astype(jnp.int32)
    fluence = jnp.clip(jnp.exp(jax.random.uniform(arg_keys[2], (NZONE,), jnp.float32, math.log(5.0), math.log(40.0))), 5.0, 40.0)
    seed_adjoint = gaussian(arg_keys[3], (NZ, ROWS, NC), 1.0, 6.0, ((0, 4), (2, 32)), jnp.float32)
    return dict(stored_energy_density=stored_energy_density, zones=zones, fluence=fluence, seed_adjoint=seed_adjoint)


melt_level = 1.0
latent_heat = 1.0
smooth_width = 0.1
resting_diffusivity_level = 0.6
peak_diffusivity_level = 0.8
absorb_solid = 0.004
absorb_liquid = 0.03
wafer_drain_rate = 0.5
time_step = 0.1

def silicon_constants(stored_energy_density):
    lower = (stored_energy_density - melt_level) / smooth_width
    upper = (stored_energy_density - melt_level - latent_heat) / smooth_width
    phase_change_ramp = smooth_width * (jax.nn.softplus(lower) - jax.nn.softplus(upper))
    kelvin_distribution = stored_energy_density - phase_change_ramp
    diffusive_transport_coefficient = resting_diffusivity_level + peak_diffusivity_level / (1.0 + kelvin_distribution * kelvin_distribution)
    optical_capture_share = absorb_solid + (absorb_liquid - absorb_solid) * phase_change_ramp / latent_heat
    return (kelvin_distribution, diffusive_transport_coefficient, optical_capture_share)

def edge_energy_current(kelvin_distribution, diffusive_transport_coefficient, axis_orientation):
    number_of_voxels = kelvin_distribution.shape[axis_orientation]
    solidus_kelvin_value = lax.slice_in_dim(kelvin_distribution, 0, number_of_voxels - 1, axis=axis_orientation)
    liquidus_kelvin_value = lax.slice_in_dim(kelvin_distribution, 1, number_of_voxels, axis=axis_orientation)
    diffusivity_floor = lax.slice_in_dim(diffusive_transport_coefficient, 0, number_of_voxels - 1, axis=axis_orientation)
    diffusivity_ceiling = lax.slice_in_dim(diffusive_transport_coefficient, 1, number_of_voxels, axis=axis_orientation)
    return 0.5 * (diffusivity_floor + diffusivity_ceiling) * (liquidus_kelvin_value - solidus_kelvin_value)

def net_outflow_rate(flux, axis_orientation):
    widths = [(0, 0)] * flux.ndim
    widths[axis_orientation] = (1, 1)
    padded = jnp.pad(flux, widths)
    number_of_voxels = flux.shape[axis_orientation] + 1
    return lax.slice_in_dim(padded, 1, number_of_voxels + 1, axis=axis_orientation) - lax.slice_in_dim(padded, 0, number_of_voxels, axis=axis_orientation)

def advance(stored_energy_density, fluence, zone_table):
    kelvin_distribution, diffusive_transport_coefficient, optical_capture_share = silicon_constants(stored_energy_density)
    deposited_power_density = net_outflow_rate(edge_energy_current(kelvin_distribution, diffusive_transport_coefficient, 0), 0)
    deposited_power_density = deposited_power_density + net_outflow_rate(edge_energy_current(kelvin_distribution, diffusive_transport_coefficient, 2), 2)
    deposited_power_density = deposited_power_density + net_outflow_rate(edge_energy_current(kelvin_distribution, diffusive_transport_coefficient, 1), 1)
    layer = jnp.arange(NZ)
    bottom_voxel_layer = (layer == NZ - 1).astype(jnp.float32)[:, None, None]
    deposited_power_density = deposited_power_density - wafer_drain_rate * bottom_voxel_layer * kelvin_distribution
    shade = jnp.cumsum(optical_capture_share, axis=0) - optical_capture_share
    intensity = lax.optimization_barrier(jnp.sum(zone_table * fluence[:, None, None], axis=0))
    source = intensity[None] * jnp.exp(-shade) * (1.0 - jnp.exp(-optical_capture_share))
    return stored_energy_density + time_step * (deposited_power_density + source)

def reference(stored_energy_density, zones, fluence, seed_adjoint):
    zone_table = (zones[None] == jnp.arange(NZONE)[:, None, None]).astype(jnp.float32)
    states = [stored_energy_density]
    for step in range(STEPS - 1):
        states.append(advance(states[-1], fluence, zone_table))
    adjoint = seed_adjoint
    fluence_grad = jnp.zeros_like(fluence)
    for state in reversed(states):
        _, pullback = jax.vjp(partial(advance, zone_table=zone_table), state, fluence)
        adjoint, step_grad = pullback(adjoint)
        fluence_grad = fluence_grad + step_grad
    return (adjoint, fluence_grad)
```

```python
import math

import jax
import jax.numpy as jnp
from jax import lax
from jax.experimental import pallas as pl
from jax.experimental.pallas import tpu as pltpu
from jax.sharding import PartitionSpec as P


NZONE = 16
CORE = 32
HALO = 8
WIDE = CORE + 2 * HALO
SEED_HALO = 4
SEED_WIDE = CORE + 2 * SEED_HALO
BASE = 8
HIGH = WIDE + 2 * BASE
DT = 0.1
ABSORB_SOLID = 0.004
ABSORB_RISE = 0.026
LOG2E = math.log2(math.e)
EM10 = math.exp(-10.0)
F32 = jnp.float32


def _params():
    return pltpu.CompilerParams(vmem_limit_bytes=16 * 1024 * 1024)


def _vmem(*shape):
    return pltpu.VMEM(shape, F32)


def _full():
    return pl.BlockSpec(memory_space=pltpu.VMEM)


def _smem():
    return pl.BlockSpec(memory_space=pltpu.SMEM)


def _lanes(rows):
    return lax.broadcasted_iota(jnp.int32, (rows, 128), 1)


def _packed(ref, g):
    rows = [ref[8 * sub + g] for sub in range(4)]
    return jnp.concatenate(rows, axis=0).T


def pack_state(d_ref, fluence_ref, h_ref, zones_ref, own, to1, to2, to3, edge, light, zid, light_own, buf, lbuf):
    d = d_ref[0]
    zero = jnp.zeros((HALO, 128), F32)
    for g in range(8):
        buf[g, 0:HALO] = zero
        buf[g, HALO + 128 :] = zero
        packed = _packed(h_ref, g)
        buf[g, HALO : HALO + 128] = packed
        edge[0, g] = packed[0:HALO]
        edge[1, g] = packed[128 - HALO :]
    for k, out in enumerate((own, to1, to2, to3)):
        start = pl.multiple_of(lax.rem(d + k, 4) * CORE, CORE)
        out[...] = buf[:, pl.ds(start, WIDE)]
    zones = zones_ref[...]
    intensity = jnp.zeros(zones.shape, F32)
    for k in range(NZONE):
        intensity = jnp.where(zones == k, fluence_ref[k] * DT, intensity)
    packed = jnp.concatenate([intensity] * 4, axis=0).T
    light[...] = packed
    lbuf[0:HALO] = zero
    lbuf[HALO : HALO + 128] = packed
    lbuf[HALO + 128 :] = zero
    start = pl.multiple_of(d * CORE, CORE)
    light_own[...] = lbuf[pl.ds(start, WIDE)]
    lbuf[0:128] = jnp.concatenate([zones.astype(F32)] * 4, axis=0).T
    zid[...] = lbuf[pl.ds(start, CORE)]


def pack_seed(d_ref, a_ref, edge, light, own, to1, to2, to3, e0, e1, e2, e3, buf, ebuf):
    d = d_ref[0]
    zero = jnp.zeros((SEED_HALO, 128), F32)
    for g in range(8):
        buf[g, 0:SEED_HALO] = zero
        buf[g, SEED_HALO + 128 :] = zero
        packed = _packed(a_ref, g)
        buf[g, SEED_HALO : SEED_HALO + 128] = packed
        ebuf[0, g, 0:8] = edge[0, g]
        ebuf[1, g, 0:8] = edge[1, g]
        ebuf[0, g, 8:12] = packed[0:4]
        ebuf[1, g, 8:12] = packed[124:128]
        part = 4 * (g % 2)
        ebuf[0, g, 12:16] = light[part : part + 4]
        ebuf[1, g, 12:16] = light[120 + part : 124 + part]
    for k, out in enumerate((own, to1, to2, to3)):
        start = pl.multiple_of(lax.rem(d + k, 4) * CORE, CORE)
        out[...] = buf[:, pl.ds(start, SEED_WIDE)]
    for j, out in enumerate((e0, e1, e2, e3)):
        last = (d == (-j) % 4).astype(jnp.int32)
        out[...] = ebuf[last]


def _rows_of(start, count):
    return pl.ds(BASE + start, count)


def _prefix(total, lane):
    below1 = jnp.where(lane >= 32, pltpu.roll(total, 32, 1), 0.0)
    below2 = jnp.where(lane >= 64, pltpu.roll(total, 64, 1), 0.0)
    below3 = jnp.where(lane >= 96, pltpu.roll(total, 96, 1), 0.0)
    return below1 + below2 + below3


def _suffix(total, lane):
    above1 = jnp.where(lane < 96, pltpu.roll(total, 96, 1), 0.0)
    above2 = jnp.where(lane < 64, pltpu.roll(total, 64, 1), 0.0)
    above3 = jnp.where(lane < 32, pltpu.roll(total, 32, 1), 0.0)
    return above1 + above2 + above3


def _all_subs(total):
    pair = total + pltpu.roll(total, 32, 1)
    return pair + pltpu.roll(pair, 64, 1)


def _properties(n, h_ref, t_ref, k_ref, c_ref, r_ref, l_ref, first, count):
    span = _rows_of(first, count)
    lane = _lanes(count)

    def slab(s, carry):
        run = jnp.zeros((count, 128), F32)
        for g in range(8):
            i = s * 8 + g
            h = h_ref[i, span]
            e = jnp.exp2(h * (10.0 * LOG2E) - 10.0 * LOG2E)
            u = 1.0 + e
            v = 1.0 + EM10 * e
            inv = pl.reciprocal(u * v)
            ramp = 0.1 * jnp.log(u * (u * inv))
            t = h - ramp
            m = pl.reciprocal(1.0 + t * t)
            t_ref[n, i, span] = t
            k_ref[n, i, span] = 0.03 + 0.04 * m
            c_ref[n, i, span] = (-0.08 * t) * (m * m)
            r_ref[n, i, span] = e * ((1.0 - EM10) * inv)
            l_ref[n, s * 9 + g, span] = run
            run = run + (ABSORB_SOLID + ABSORB_RISE * ramp)
        above = carry + _prefix(run, lane)
        for g in range(8):
            at = s * 9 + g
            l_ref[n, at, span] = jnp.exp(-(above + l_ref[n, at, span]))
        l_ref[n, s * 9 + 8, span] = jnp.exp(-(above + run))
        return carry + _all_subs(run)

    lax.fori_loop(0, 4, slab, jnp.zeros((count, 128), F32))


def _ghost(ref_rows, lat, d):
    @pl.when(jnp.logical_and(lat == 0, d == 0))
    def _():
        for i in range(32):
            ref_rows(i, HALO - 1)[...] = ref_rows(i, HALO)[...]

    @pl.when(jnp.logical_and(lat == 31, d == 3))
    def _():
        for i in range(32):
            ref_rows(i, HALO + CORE)[...] = ref_rows(i, HALO + CORE - 1)[...]


def _later(load, s, lane):
    here, after = load(s * 8), load(jnp.minimum(s + 1, 3) * 8)
    return pltpu.roll(jnp.where(lane < 32, after, here), 96, 1)


def _earlier(load, s, lane):
    here, before = load(s * 8 + 7), load(jnp.maximum(s - 1, 0) * 8 + 7)
    return pltpu.roll(jnp.where(lane >= 96, before, here), 32, 1)


def _advance(n, h_ref, new_ref, t_ref, k_ref, l_ref, light, first, count):
    span = _rows_of(first, count)
    up, down = _rows_of(first + 1, count), _rows_of(first - 1, count)
    lane = _lanes(count)
    inside = jnp.where(lax.rem(lane, 32) == 31, 0.0, 1.0)

    def slab(s, carry):
        bottom = jnp.logical_and(lane >= 96, s == 3)
        top = jnp.logical_and(lane < 32, s == 0)
        load_t = lambda i: t_ref[n, i, span]
        load_k = lambda i: k_ref[n, i, span]
        t0, k0 = load_t(s * 8), load_k(s * 8)
        t_before, k_before = _earlier(load_t, s, lane), _earlier(load_k, s, lane)
        flux_before = jnp.where(top, 0.0, (k0 + k_before) * (t0 - t_before))
        for g in range(8):
            i = s * 8 + g
            if g < 7:
                t1, k1 = load_t(i + 1), load_k(i + 1)
                flux = (k0 + k1) * (t1 - t0)
            else:
                t1, k1 = _later(load_t, s, lane), _later(load_k, s, lane)
                flux = jnp.where(bottom, -0.05 * t0, (k0 + k1) * (t1 - t0))
            change = flux - flux_before
            across = (k0 + pltpu.roll(k0, 127, 1)) * (pltpu.roll(t0, 127, 1) - t0) * inside
            change = change + (across - pltpu.roll(across, 1, 1))
            t_up, t_down = t_ref[n, i, up], t_ref[n, i, down]
            k_up, k_down = k_ref[n, i, up], k_ref[n, i, down]
            change = change + ((k0 + k_up) * (t_up - t0) - (k0 + k_down) * (t0 - t_down))
            source = light[span] * (l_ref[n, s * 9 + g, span] - l_ref[n, s * 9 + g + 1, span])
            new_ref[i, span] = h_ref[i, span] + (change + source)
            t0, k0, flux_before = t1, k1, flux
        return carry

    lax.fori_loop(0, 4, slab, 0)


def forward(where, own, r1, r2, r3, e0, e1, e2, e3, light_own, t_ref, k_ref, c_ref, r_ref, l_ref, light, ha, hb):
    lat, d = where[0], where[1]
    for k, block in enumerate((own, r1, r2, r3)):
        source = lax.rem(d + 4 - k, 4) * 8
        ha[pl.ds(source, 8), _rows_of(0, WIDE)] = block[...]
    light[0:BASE] = jnp.zeros((BASE, 128), F32)
    light[BASE + WIDE :] = jnp.zeros((BASE, 128), F32)
    light[_rows_of(0, WIDE)] = light_own[...]

    @pl.when(d == 0)
    def _():
        for j, e in enumerate((e0, e1, e2, e3)):
            ha[pl.ds(((-j) % 4) * 8, 8), _rows_of(0, 8)] = e[:, 0:8]
        light[_rows_of(0, 4)] = e0[0, 12:16]
        light[_rows_of(4, 4)] = e0[1, 12:16]

    @pl.when(d == 3)
    def _():
        for j, e in enumerate((e0, e1, e2, e3)):
            ha[pl.ds(((3 - j) % 4) * 8, 8), _rows_of(HALO + CORE, 8)] = e[:, 0:8]
        light[_rows_of(HALO + CORE, 4)] = e0[0, 12:16]
        light[_rows_of(HALO + CORE + 4, 4)] = e0[1, 12:16]

    source, target = ha, hb
    for n in range(4):
        first, count = (0, WIDE) if n < 3 else (SEED_HALO, SEED_WIDE)
        _properties(n, source, t_ref, k_ref, c_ref, r_ref, l_ref, first, count)
        if n < 3:
            _ghost(lambda i, c, n=n: t_ref.at[n, i, pl.ds(BASE + c, 1)], lat, d)
            first, count = (0, WIDE) if n < 2 else (SEED_HALO, SEED_WIDE)
            _advance(n, source, target, t_ref, k_ref, l_ref, light, first, count)
            source, target = target, source


def _retreat(n, a_ref, new_ref, t_ref, k_ref, c_ref, r_ref, l_ref, light, run_ref, first, count):
    span = _rows_of(first, count)
    up, down = _rows_of(first + 1, count), _rows_of(first - 1, count)
    lane = _lanes(count)
    inside = jnp.where(lax.rem(lane, 32) == 31, 0.0, 1.0)
    rows = pl.ds(0, count)
    gain = ABSORB_RISE * light[span]

    def slab(step, state):
        s = 3 - step
        carry, seen = state
        run = jnp.zeros((count, 128), F32)
        for g in reversed(range(8)):
            run_ref[g, rows] = run
            lost = l_ref[n, s * 9 + g, span] - l_ref[n, s * 9 + g + 1, span]
            run = run + a_ref[s * 8 + g, span] * lost
        below = carry + _suffix(run, lane)
        bottom = jnp.logical_and(lane >= 96, s == 3)
        top = jnp.logical_and(lane < 32, s == 0)
        load_a = lambda i: a_ref[i, span]
        load_t = lambda i: t_ref[n, i, span]
        load_k = lambda i: k_ref[n, i, span]
        a0, t0, k0 = load_a(s * 8), load_t(s * 8), load_k(s * 8)
        jump = jnp.where(top, 0.0, _earlier(load_a, s, lane) - a0)
        push_before = jump * (_earlier(load_k, s, lane) + k0)
        share_before = jump * (t0 - _earlier(load_t, s, lane))
        for g in range(8):
            i = s * 8 + g
            if g < 7:
                a1, t1, k1 = load_a(i + 1), load_t(i + 1), load_k(i + 1)
                jump = a0 - a1
                push = jump * (k0 + k1)
                share = jump * (t1 - t0)
            else:
                a1, t1, k1 = _later(load_a, s, lane), _later(load_t, s, lane), _later(load_k, s, lane)
                jump = a0 - a1
                push = jnp.where(bottom, 0.05 * a0, jump * (k0 + k1))
                share = jnp.where(bottom, 0.0, jump * (t1 - t0))
            grad_t = push_before - push
            grad_k = share_before + share
            jump = (a0 - pltpu.roll(a0, 127, 1)) * inside
            push_r = jump * (k0 + pltpu.roll(k0, 127, 1))
            share_r = jump * (pltpu.roll(t0, 127, 1) - t0)
            grad_t = grad_t + (pltpu.roll(push_r, 1, 1) - push_r)
            grad_k = grad_k + (pltpu.roll(share_r, 1, 1) + share_r)
            jump_up = a0 - a_ref[i, up]
            jump_down = a_ref[i, down] - a0
            grad_t = grad_t + (jump_down * (k_ref[n, i, down] + k0) - jump_up * (k0 + k_ref[n, i, up]))
            grad_k = grad_k + (jump_down * (t0 - t_ref[n, i, down]) + jump_up * (t_ref[n, i, up] - t0))
            heat = grad_t + c_ref[n, i, span] * grad_k
            absorbed = gain * (a0 * l_ref[n, s * 9 + g + 1, span] - (below + run_ref[g, rows]))
            new_ref[i, span] = a0 + (heat + r_ref[n, i, span] * (absorbed - heat))
            a0, t0, k0, push_before, share_before = a1, t1, k1, push, share
        return (carry + _all_subs(run), seen + run)

    zero = jnp.zeros((count, 128), F32)
    return lax.fori_loop(0, 4, slab, (zero, zero))[1]


def backward(where, own, r1, r2, r3, e0, e1, e2, e3, t_ref, k_ref, c_ref, r_ref, l_ref, light, zid, a_ref, zpart, ab, run_ref):
    lat, d = where[0], where[1]
    aa = a_ref
    for k, block in enumerate((own, r1, r2, r3)):
        source = lax.rem(d + 4 - k, 4) * 8
        ab[pl.ds(source, 8), _rows_of(SEED_HALO, SEED_WIDE)] = block[...]

    @pl.when(d == 0)
    def _():
        for j, e in enumerate((e0, e1, e2, e3)):
            ab[pl.ds(((-j) % 4) * 8, 8), _rows_of(SEED_HALO, 4)] = e[:, 8:12]

    @pl.when(d == 3)
    def _():
        for j, e in enumerate((e0, e1, e2, e3)):
            ab[pl.ds(((3 - j) % 4) * 8, 8), _rows_of(HALO + CORE, 4)] = e[:, 8:12]

    source, target = ab, aa
    total = jnp.zeros((CORE, 128), F32)
    for n in (3, 2, 1):
        _ghost(lambda i, c, ref=source: ref.at[i, pl.ds(BASE + c, 1)], lat, d)
        seen = _retreat(n, source, target, t_ref, k_ref, c_ref, r_ref, l_ref, light, run_ref, SEED_HALO, SEED_WIDE)
        total = total + seen[HALO - SEED_HALO : HALO - SEED_HALO + CORE]
        source, target = target, source
    _ghost(lambda i, c, ref=source: ref.at[i, pl.ds(BASE + c, 1)], lat, d)
    span = _rows_of(HALO, CORE)

    def slab(s, total):
        for g in range(8):
            at = s * 9 + g
            total = total + source[s * 8 + g, span] * (l_ref[0, at, span] - l_ref[0, at + 1, span])
        return total

    total = lax.fori_loop(0, 4, slab, total) * DT
    zones = zid[...]
    for k in range(NZONE):
        zpart[k : k + 1] = jnp.sum(jnp.where(zones == float(k), total, 0.0), axis=0, keepdims=True)


def last_step(where, a_ref, t_ref, k_ref, c_ref, r_ref, l_ref, light, own, to1, to2, to3, new_ref, run_ref):
    d = where[1]
    _retreat(0, a_ref, new_ref, t_ref, k_ref, c_ref, r_ref, l_ref, light, run_ref, HALO, CORE)
    for k, out in enumerate((own, to1, to2, to3)):
        out[...] = new_ref[pl.ds(lax.rem(d + k, 4) * 8, 8), _rows_of(HALO, CORE)]


def unpack(where, own, r1, r2, r3, out, buf):
    d = where[1]
    for k, block in enumerate((own, r1, r2, r3)):
        start = pl.multiple_of(lax.rem(d + 4 - k, 4) * CORE, CORE)
        buf[:, pl.ds(start, CORE)] = block[...]
    for g in range(8):
        plain = buf[g].T
        for sub in range(4):
            out[8 * sub + g] = plain[32 * sub : 32 * sub + 32]


def _around(x, k):
    return lax.ppermute(x, "dep", [(s, (s + k) % 4) for s in range(4)])


def _edges(x, j):
    pairs = [(l * 4 + (-j) % 4, (l + 1) * 4) for l in range(31)]
    pairs += [(l * 4 + (3 - j) % 4, (l - 1) * 4 + 3) for l in range(1, 32)]
    return lax.ppermute(x, ("lat", "dep"), pairs)


def _place(y, z, core, x):
    return ((y * 4 + z) * 2 + core) * 4 + x


def _meet(v, partner):
    pairs = []
    for y in range(4):
        for z in range(4):
            for core in range(2):
                for x in range(4):
                    pairs.append((_place(y, z, core, x), _place(*partner(y, z, core, x))))
    return v + lax.ppermute(v, ("lat", "dep"), pairs)


def total_of(v):
    for partner in (
        lambda y, z, core, x: (y, z, 1 - core, x),
        lambda y, z, core, x: (y, z ^ 1, core, x),
        lambda y, z, core, x: (y, 3 - z, core, x),
        lambda y, z, core, x: (y ^ 1, z, core, x),
        lambda y, z, core, x: (3 - y, z, core, x),
        lambda y, z, core, x: (y, z, core, x ^ 1),
        lambda y, z, core, x: (y, z, core, 3 - x),
    ):
        v = _meet(v, partner)
    return v


def _shape(*dims):
    return jax.ShapeDtypeStruct(dims, F32)


def per_device(h, zones, fluence, seed):
    d = lax.axis_index("dep")
    where = jnp.stack([lax.axis_index("lat"), d]).astype(jnp.int32)
    dep = d.astype(jnp.int32)[None]
    block = _shape(8, WIDE, 128)
    h_own, h1, h2, h3, edge, light, zid, light_own = pl.pallas_call(
        pack_state,
        out_shape=(block,) * 4 + (_shape(2, 8, 8, 128), _shape(128, 128), _shape(CORE, 128), _shape(WIDE, 128)),
        in_specs=[_smem(), _smem(), _full(), _full()],
        out_specs=(_full(),) * 8,
        scratch_shapes=[_vmem(8, 128 + 2 * HALO, 128), _vmem(128 + 2 * HALO, 128)],
        compiler_params=_params(),
        name="pack_state",
    )(dep, fluence, h, zones)
    h2, h1, h3 = _around(h2, 2), _around(h1, 1), _around(h3, 3)
    seed_block = _shape(8, SEED_WIDE, 128)
    edge_block = _shape(8, 16, 128)
    s_own, s1, s2, s3, *e = pl.pallas_call(
        pack_seed,
        out_shape=(seed_block,) * 4 + (edge_block,) * 4,
        in_specs=[_smem()] + [_full()] * 3,
        out_specs=(_full(),) * 8,
        scratch_shapes=[_vmem(8, 128 + 2 * SEED_HALO, 128), _vmem(2, 8, 16, 128)],
        compiler_params=_params(),
        name="pack_seed",
    )(dep, seed, edge, light)
    e = [_edges(e[j], j) for j in range(4)]
    s2, s1, s3 = _around(s2, 2), _around(s1, 1), _around(s3, 3)
    field = pltpu.VMEM((4, 32, HIGH, 128), F32)
    shade = pltpu.VMEM((4, 36, HIGH, 128), F32)
    states = pl.pallas_call(
        forward,
        out_shape=(field,) * 4 + (shade, pltpu.VMEM((HIGH, 128), F32)),
        in_specs=[_smem()] + [_full()] * 9,
        out_specs=(_full(),) * 6,
        scratch_shapes=[_vmem(32, HIGH, 128)] * 2,
        compiler_params=_params(),
        name="forward",
    )(where, h_own, h1, h2, h3, *e, light_own)
    a, zpart = pl.pallas_call(
        backward,
        out_shape=(pltpu.VMEM((32, HIGH, 128), F32), _shape(NZONE, 128)),
        in_specs=[_smem()] + [_full()] * 15,
        out_specs=(_full(),) * 2,
        scratch_shapes=[_vmem(32, HIGH, 128), _vmem(8, SEED_WIDE, 128)],
        compiler_params=_params(),
        name="backward",
    )(where, s_own, s1, s2, s3, *e, *states, zid)
    piece = _shape(8, CORE, 128)
    o_own, o1, o2, o3 = pl.pallas_call(
        last_step,
        out_shape=(piece,) * 4,
        in_specs=[_smem()] + [_full()] * 7,
        out_specs=(_full(),) * 4,
        scratch_shapes=[_vmem(32, HIGH, 128), _vmem(8, CORE, 128)],
        compiler_params=_params(),
        name="last_step",
    )(where, a, *states)
    o2, o1, o3 = _around(o2, 2), _around(o1, 1), _around(o3, 3)
    total = jnp.sum(total_of(zpart), axis=1)
    out = pl.pallas_call(
        unpack,
        out_shape=_shape(32, 32, 128),
        in_specs=[_smem()] + [_full()] * 4,
        out_specs=_full(),
        scratch_shapes=[_vmem(8, 128, 128)],
        compiler_params=_params(),
        name="unpack",
    )(where, o_own, o1, o2, o3)
    return out, total


def solution(mesh):
    in_specs = (P("dep", None, "lat"), P(None, "lat"), P(), P("dep", None, "lat"))
    out_specs = (P("dep", None, "lat"), P())
    return jax.shard_map(per_device, mesh=mesh, in_specs=in_specs, out_specs=out_specs, check_vma=False)
```

```python
import math

import jax
import jax.numpy as jnp
from jax import lax
from jax.experimental import pallas as pl
from jax.experimental.pallas import tpu as pltpu
from jax.sharding import PartitionSpec as P


NZONE = 16
CORE = 32
HALO = 8
WIDE = CORE + 2 * HALO
SEED_HALO = 4
SEED_WIDE = CORE + 2 * SEED_HALO
BASE = 8
HIGH = WIDE + 2 * BASE
DT = 0.1
ABSORB_SOLID = 0.004
ABSORB_RISE = 0.026
LOG2E = math.log2(math.e)
EM10 = math.exp(-10.0)
F32 = jnp.float32


def _params():
    return pltpu.CompilerParams(vmem_limit_bytes=16 * 1024 * 1024)


def _vmem(*shape):
    return pltpu.VMEM(shape, F32)


def _full():
    return pl.BlockSpec(memory_space=pltpu.VMEM)


def _any():
    return pl.BlockSpec(memory_space=pl.ANY)


def _lanes():
    return lax.broadcasted_iota(jnp.int32, (8, 128), 1)


def _packed(ref, g, d):
    tiles = []
    for p in range(4):
        rf = lax.rem(p + 4 - d, 4)
        tiles += [ref[8 * sub + g, pl.ds(rf, 8, stride=4)] for sub in range(4)]
    return jnp.concatenate(tiles, axis=0).T


def _surface(ref, rf):
    return jnp.concatenate([ref[pl.ds(rf, 8, stride=4)]] * 16, axis=0).T


def pack(fluence_in, h_in, zones_in, a_in, state, seed, light, zid, to_right, to_left, h, a, zones, flat, zbuf, fluence, sems):
    d = lax.axis_index("dep")
    copies = [
        pltpu.make_async_copy(source, target, sems.at[k])
        for k, (source, target) in enumerate(((h_in, h), (zones_in, zones), (fluence_in, fluence), (a_in, a)))
    ]
    for copy in copies:
        copy.start()
    copies[0].wait()
    for g in range(8):
        packed = _packed(h, g, d)
        state[g] = packed
        to_left[g, 0:8] = packed[0:8]
        to_right[g, 0:8] = packed[120:128]
    copies[1].wait()
    copies[2].wait()
    ids = zones[...]
    intensity = jnp.zeros(ids.shape, F32)
    for k in range(NZONE):
        intensity = jnp.where(ids == k, fluence[k] * DT, intensity)
    flat[0] = intensity
    flat[1] = ids.astype(F32)
    start = pl.multiple_of(d * CORE, CORE)
    for rf in range(4):
        packed = _surface(flat.at[0], rf)
        light[rf] = packed
        for half in range(2):
            to_left[2 * rf + half, 12:16] = packed[4 * half : 4 * half + 4]
            to_right[2 * rf + half, 12:16] = packed[120 + 4 * half : 124 + 4 * half]
        zbuf[...] = _surface(flat.at[1], rf)
        zid[rf] = zbuf[pl.ds(start, CORE)]
    copies[3].wait()
    for g in range(8):
        packed = _packed(a, g, d)
        seed[g] = packed
        to_left[g, 8:12] = packed[0:4]
        to_right[g, 8:12] = packed[124:128]


def insert(state, seed, light, left, right, h0, h1, h2, h3, s0, s1, s2, s3, light_own, hbuf, sbuf, lbuf):
    d = lax.axis_index("dep")
    hbuf[:, 0:8] = left[:, 0:8]
    hbuf[:, 8:136] = state[...]
    hbuf[:, 136:144] = right[:, 0:8]
    for k, out in enumerate((h0, h1, h2, h3)):
        start = pl.multiple_of(lax.rem(d + k, 4) * CORE, CORE)
        out[...] = hbuf[:, pl.ds(start, WIDE)]
    sbuf[:, 0:4] = left[:, 8:12]
    sbuf[:, 4:132] = seed[...]
    sbuf[:, 132:136] = right[:, 8:12]
    for k, out in enumerate((s0, s1, s2, s3)):
        start = pl.multiple_of(lax.rem(d + k, 4) * CORE, CORE)
        out[...] = sbuf[:, pl.ds(start, SEED_WIDE)]
    start = pl.multiple_of(d * CORE, CORE)
    for rf in range(4):
        for half in range(2):
            lbuf[4 * half : 4 * half + 4] = left[2 * rf + half, 12:16]
            lbuf[136 + 4 * half : 140 + 4 * half] = right[2 * rf + half, 12:16]
        lbuf[8:136] = light[rf]
        light_own[rf] = lbuf[pl.ds(start, WIDE)]


def _source_masks():
    part = lax.rem(_lanes() // 32 + 4 - lax.axis_index("dep"), 4)
    return [part == j for j in range(4)]


def _pick(masks, shift, values):
    return jnp.where(
        masks[shift % 4],
        values[0],
        jnp.where(masks[(shift + 1) % 4], values[1], jnp.where(masks[(shift + 2) % 4], values[2], values[3])),
    )


def _gather(blocks, field, first, count):
    masks = _source_masks()

    def tile(i, carry):
        g, c = i // (count // 8), pl.multiple_of(lax.rem(i, count // 8) * 8, 8)
        own, r1, r2, r3 = [block[g, pl.ds(c, 8)] for block in blocks]
        for rf in range(4):
            mixed = _pick(masks, rf, (own, r3, r2, r1))
            field[8 * rf + g, pl.ds(BASE + first + c, 8)] = mixed if rf == 0 else pltpu.roll(mixed, 128 - 32 * rf, 1)
        return carry

    lax.fori_loop(0, count, tile, 0, unroll=2)


class _Tiles:
    def __init__(self, row):
        self.here, self.up, self.down = pl.ds(row, 8), pl.ds(row + 1, 8), pl.ds(row - 1, 8)


def _inclusive(total, lane, reverse):
    for step in (8, 16, 32, 64):
        if reverse:
            total = total + jnp.where(lane < 128 - step, pltpu.roll(total, 128 - step, 1), 0.0)
        else:
            total = total + jnp.where(lane >= step, pltpu.roll(total, step, 1), 0.0)
    return total


def _properties(n, rf, tiles, states, t_ref, k_ref, c_ref, r_ref, l_ref):
    lane = _lanes()
    here = tiles.here
    run = jnp.zeros((8, 128), F32)
    runs = []
    for g in range(8):
        i = 8 * rf + g
        h = states[g]
        e = jnp.exp2(h * (10.0 * LOG2E) - 10.0 * LOG2E)
        u = 1.0 + e
        v = 1.0 + EM10 * e
        inv = pl.reciprocal(u * v)
        ramp = 0.1 * jnp.log(u * (u * inv))
        t = h - ramp
        m = pl.reciprocal(1.0 + t * t)
        t_ref[n, i, here] = t
        k_ref[n, i, here] = 0.03 + 0.04 * m
        c_ref[n, i, here] = (-0.08 * t) * (m * m)
        r_ref[n, i, here] = e * ((1.0 - EM10) * inv)
        runs.append(run)
        run = run + (ABSORB_SOLID * LOG2E + (ABSORB_RISE * LOG2E) * ramp)
    above = _inclusive(run, lane, False) - run
    for g in range(8):
        l_ref[n, 9 * rf + g, here] = jnp.exp2(-(above + runs[g]))
    l_ref[n, 9 * rf + 8, here] = jnp.exp2(-(above + run))


def _advance(n, tiles, h_ref, t_ref, k_ref, l_ref, light, then):
    lane = _lanes()
    inside = lax.rem(lane, 8) < 7
    above_bottom = lane < 120
    here, up, down = tiles.here, tiles.up, tiles.down

    def across(g):
        t3, k3 = t_ref[n, 24 + g, here], k_ref[n, 24 + g, here]
        t0, k0 = pltpu.roll(t_ref[n, g, here], 127, 1), pltpu.roll(k_ref[n, g, here], 127, 1)
        return jnp.where(inside, (k3 + k0) * (t0 - t3), 0.0)

    last = [across(g) for g in range(8)]
    before = [pltpu.roll(f, 1, 1) for f in last]
    for rf in range(4):
        i0 = 8 * rf
        t = [t_ref[n, i0 + g, here] for g in range(8)]
        k = [k_ref[n, i0 + g, here] for g in range(8)]
        end = jnp.where(above_bottom, (k[7] + pltpu.roll(k[0], 120, 1)) * (pltpu.roll(t[0], 120, 1) - t[7]), 0.0)
        flux_before = pltpu.roll(end, 8, 1)
        new = []
        for g in range(8):
            i = i0 + g
            if g < 7:
                flux = (k[g] + k[g + 1]) * (t[g + 1] - t[g])
            else:
                flux = jnp.where(above_bottom, end, -0.05 * t[7])
            if rf < 3:
                side = (k[g] + k_ref[n, i + 8, here]) * (t_ref[n, i + 8, here] - t[g])
            else:
                side = last[g]
            change = (flux - flux_before) + (side - before[g])
            change = change + (
                (k[g] + k_ref[n, i, up]) * (t_ref[n, i, up] - t[g])
                - (k[g] + k_ref[n, i, down]) * (t[g] - t_ref[n, i, down])
            )
            source = light[rf, here] * (l_ref[n, 9 * rf + g, here] - l_ref[n, 9 * rf + g + 1, here])
            new.append(h_ref[i, here] + (change + source))
            flux_before, before[g] = flux, side
        then(rf, new)


def _ghost(ref_rows):
    lat, d = lax.axis_index("lat"), lax.axis_index("dep")

    @pl.when(jnp.logical_and(lat == 0, d == 0))
    def _():
        for i in range(32):
            ref_rows(i, HALO - 1)[...] = ref_rows(i, HALO)[...]

    @pl.when(jnp.logical_and(lat == 31, d == 3))
    def _():
        for i in range(32):
            ref_rows(i, HALO + CORE)[...] = ref_rows(i, HALO + CORE - 1)[...]


def forward(own, r1, r2, r3, light_own, t_ref, k_ref, c_ref, r_ref, l_ref, light, ha, hb):
    _gather((own, r1, r2, r3), ha, 0, WIDE)
    for rf in range(4):
        light[rf, BASE : BASE + WIDE] = light_own[rf]
    fields = (t_ref, k_ref, c_ref, r_ref, l_ref)

    def start(c, carry):
        tiles = _Tiles(BASE + 8 * c)
        for rf in range(4):
            _properties(0, rf, tiles, [ha[8 * rf + g, tiles.here] for g in range(8)], *fields)
        return carry

    lax.fori_loop(0, WIDE // 8, start, 0)
    source, target = ha, hb
    for n in range(3):
        _ghost(lambda i, c, n=n: t_ref.at[n, i, pl.ds(BASE + c, 1)])
        first, count = (0, WIDE) if n < 2 else (SEED_HALO, SEED_WIDE)

        def chunk(c, carry, n=n, first=first, source=source, target=target):
            tiles = _Tiles(BASE + first + 8 * c)

            def then(rf, new):
                for g in range(8):
                    if n < 2:
                        target[8 * rf + g, tiles.here] = new[g]
                _properties(n + 1, rf, tiles, new, *fields)

            _advance(n, tiles, source, t_ref, k_ref, l_ref, light, then)
            return carry

        lax.fori_loop(0, count // 8, chunk, 0)
        source, target = target, source


def _retreat(n, tiles, a_ref, t_ref, k_ref, c_ref, r_ref, l_ref, light, put, seen):
    lane = _lanes()
    inside = lax.rem(lane, 8) < 7
    above_bottom = lane < 120
    here, up, down = tiles.here, tiles.up, tiles.down

    def across(g):
        a3, t3, k3 = a_ref[24 + g, here], t_ref[n, 24 + g, here], k_ref[n, 24 + g, here]
        a0, t0, k0 = [pltpu.roll(x, 127, 1) for x in (a_ref[g, here], t_ref[n, g, here], k_ref[n, g, here])]
        jump = jnp.where(inside, a3 - a0, 0.0)
        return jump * (k3 + k0), jump * (t0 - t3)

    last = [across(g) for g in range(8)]
    before = [(pltpu.roll(push, 1, 1), pltpu.roll(share, 1, 1)) for push, share in last]
    for rf in range(4):
        i0 = 8 * rf
        a = [a_ref[i0 + g, here] for g in range(8)]
        t = [t_ref[n, i0 + g, here] for g in range(8)]
        k = [k_ref[n, i0 + g, here] for g in range(8)]
        run = jnp.zeros((8, 128), F32)
        runs = [None] * 8
        for g in reversed(range(8)):
            runs[g] = run
            run = run + a[g] * (l_ref[n, 9 * rf + g, here] - l_ref[n, 9 * rf + g + 1, here])
        below = _inclusive(run, lane, True) - run
        seen(rf, run)
        gain = ABSORB_RISE * light[rf, here]
        jump = jnp.where(above_bottom, a[7] - pltpu.roll(a[0], 120, 1), 0.0)
        push_end = jump * (k[7] + pltpu.roll(k[0], 120, 1))
        share_end = jump * (pltpu.roll(t[0], 120, 1) - t[7])
        push_before, share_before = pltpu.roll(push_end, 8, 1), pltpu.roll(share_end, 8, 1)
        for g in range(8):
            i = i0 + g
            if g < 7:
                jump = a[g] - a[g + 1]
                push, share = jump * (k[g] + k[g + 1]), jump * (t[g + 1] - t[g])
            else:
                push, share = jnp.where(above_bottom, push_end, 0.05 * a[7]), share_end
            if rf < 3:
                jump = a[g] - a_ref[i + 8, here]
                push_r, share_r = jump * (k[g] + k_ref[n, i + 8, here]), jump * (t_ref[n, i + 8, here] - t[g])
            else:
                push_r, share_r = last[g]
            grad_t = (push_before - push) + (before[g][0] - push_r)
            grad_k = (share_before + share) + (before[g][1] + share_r)
            jump_up = a[g] - a_ref[i, up]
            jump_down = a_ref[i, down] - a[g]
            grad_t = grad_t + (jump_down * (k_ref[n, i, down] + k[g]) - jump_up * (k[g] + k_ref[n, i, up]))
            grad_k = grad_k + (jump_down * (t[g] - t_ref[n, i, down]) + jump_up * (t_ref[n, i, up] - t[g]))
            heat = grad_t + c_ref[n, i, here] * grad_k
            absorbed = gain * (a[g] * l_ref[n, 9 * rf + g + 1, here] - (below + runs[g]))
            put(i, a[g] + (heat + r_ref[n, i, here] * (absorbed - heat)))
            push_before, share_before, before[g] = push, share, (push_r, share_r)


def backward(own, r1, r2, r3, t_ref, k_ref, c_ref, r_ref, l_ref, light, zid, a_ref, zpart, ab, total):
    _gather((own, r1, r2, r3), ab, SEED_HALO, SEED_WIDE)
    fields = (t_ref, k_ref, c_ref, r_ref, l_ref, light)
    total[...] = jnp.zeros(total.shape, F32)
    source, target = ab, a_ref
    for n in (3, 2, 1):
        _ghost(lambda i, c, ref=source: ref.at[i, pl.ds(BASE + c, 1)])

        def chunk(c, carry, n=n, source=source, target=target):
            tiles = _Tiles(BASE + SEED_HALO + 8 * c)

            def put(i, value):
                target[i, tiles.here] = value

            def seen(rf, value):
                total[rf, tiles.here] += value

            _retreat(n, tiles, source, *fields, put, seen)
            return carry

        lax.fori_loop(0, SEED_WIDE // 8, chunk, 0)
        source, target = target, source
    _ghost(lambda i, c, ref=source: ref.at[i, pl.ds(BASE + c, 1)])
    core = pl.ds(BASE + HALO, CORE)
    sums = []
    for rf in range(4):
        value = total[rf, core]
        for g in range(8):
            value = value + source[8 * rf + g, core] * (l_ref[0, 9 * rf + g, core] - l_ref[0, 9 * rf + g + 1, core])
        sums.append(value * DT)
    for z in range(NZONE):
        picked = [jnp.where(zid[rf] == float(z), sums[rf], 0.0) for rf in range(4)]
        zpart[z : z + 1] = jnp.sum((picked[0] + picked[1]) + (picked[2] + picked[3]), axis=0, keepdims=True)


def last_step(a_ref, t_ref, k_ref, c_ref, r_ref, l_ref, light, o0, o1, o2, o3):
    masks = _source_masks()

    def chunk(c, carry):
        tiles = _Tiles(BASE + HALO + 8 * c)
        values = [None] * 32

        def put(i, value):
            values[i] = value

        _retreat(0, tiles, a_ref, t_ref, k_ref, c_ref, r_ref, l_ref, light, put, lambda rf, value: None)
        for g in range(8):
            turned = [values[g]] + [pltpu.roll(values[8 * rf + g], 32 * rf, 1) for rf in (1, 2, 3)]
            for k, out in enumerate((o0, o1, o2, o3)):
                out[g, pl.ds(pl.multiple_of(8 * c, 8), 8)] = _pick(masks, k, turned)
        return carry

    lax.fori_loop(0, CORE // 8, chunk, 0)


def unpack(own, r1, r2, r3, out, buf):
    d = lax.axis_index("dep")
    for k, block in enumerate((own, r1, r2, r3)):
        start = pl.multiple_of(lax.rem(d + 4 - k, 4) * CORE, CORE)
        buf[:, pl.ds(start, CORE)] = block[...]
    for g in range(8):
        plain = buf[g].T
        for p in range(4):
            rf = lax.rem(p + 4 - d, 4)
            for sub in range(4):
                out[8 * sub + g, pl.ds(rf, 8, stride=4)] = plain[32 * p + 8 * sub : 32 * p + 8 * sub + 8]


def _around(x, k):
    return lax.ppermute(x, "dep", [(s, (s + k) % 4) for s in range(4)])


def _place(y, z, core, x):
    return ((y * 4 + z) * 2 + core) * 4 + x


def _meet(v, partner):
    pairs = []
    for y in range(4):
        for z in range(4):
            for core in range(2):
                for x in range(4):
                    pairs.append((_place(y, z, core, x), _place(*partner(y, z, core, x))))
    return v + lax.ppermute(v, ("lat", "dep"), pairs)


def total_of(v):
    for partner in (
        lambda y, z, core, x: (y, z, 1 - core, x),
        lambda y, z, core, x: (y, z ^ 1, core, x),
        lambda y, z, core, x: (y, 3 - z, core, x),
        lambda y, z, core, x: (y ^ 1, z, core, x),
        lambda y, z, core, x: (3 - y, z, core, x),
        lambda y, z, core, x: (y, z, core, x ^ 1),
        lambda y, z, core, x: (y, z, core, 3 - x),
    ):
        v = _meet(v, partner)
    return v


def _shape(*dims):
    return jax.ShapeDtypeStruct(dims, F32)


def _call(kernel, inputs, outs, scratch=(), spaces=None):
    return pl.pallas_call(
        kernel,
        out_shape=tuple(outs),
        in_specs=spaces or [_full()] * len(inputs),
        out_specs=(_full(),) * len(outs),
        scratch_shapes=list(scratch),
        compiler_params=_params(),
        name=kernel.__name__,
    )(*inputs)


def per_device(h, zones, fluence, seed):
    slab = _shape(8, 128, 128)
    edge = _shape(8, 16, 128)
    state, start, light, zid, to_right, to_left = _call(
        pack,
        (fluence, h, zones, seed),
        (slab, slab, _shape(4, 128, 128), _shape(4, CORE, 128), edge, edge),
        (
            _vmem(32, 32, 128),
            _vmem(32, 32, 128),
            pltpu.VMEM((32, 128), jnp.int32),
            _vmem(2, 32, 128),
            _vmem(128, 128),
            pltpu.SMEM((NZONE,), F32),
            pltpu.SemaphoreType.DMA((4,)),
        ),
        [_any()] * 4,
    )
    left = lax.ppermute(to_right, "lat", [(l, l + 1) for l in range(31)])
    right = lax.ppermute(to_left, "lat", [(l + 1, l) for l in range(31)])
    block, seed_block = _shape(8, WIDE, 128), _shape(8, SEED_WIDE, 128)
    h0, h1, h2, h3, s0, s1, s2, s3, light_own = _call(
        insert,
        (state, start, light, left, right),
        (block,) * 4 + (seed_block,) * 4 + (_shape(4, WIDE, 128),),
        (_vmem(8, 144, 128), _vmem(8, 136, 128), _vmem(144, 128)),
    )
    h2, h1, h3 = _around(h2, 2), _around(h1, 1), _around(h3, 3)
    s2, s1, s3 = _around(s2, 2), _around(s1, 1), _around(s3, 3)
    field = _vmem(4, 32, HIGH, 128)
    states = _call(
        forward,
        (h0, h1, h2, h3, light_own),
        (field,) * 4 + (_vmem(4, 36, HIGH, 128), _vmem(4, HIGH, 128)),
        [_vmem(32, HIGH, 128)] * 2,
    )
    a, zpart = _call(
        backward,
        (s0, s1, s2, s3, *states, zid),
        (_vmem(32, HIGH, 128), _shape(NZONE, 128)),
        (_vmem(32, HIGH, 128), _vmem(4, HIGH, 128)),
    )
    piece = _shape(8, CORE, 128)
    o0, o1, o2, o3 = _call(last_step, (a, *states), (piece,) * 4)
    o2, o1, o3 = _around(o2, 2), _around(o1, 1), _around(o3, 3)
    total = jnp.sum(total_of(zpart), axis=1)
    (out,) = _call(unpack, (o0, o1, o2, o3), (_shape(32, 32, 128),), (_vmem(8, 128, 128),))
    return out, total


def solution(mesh):
    in_specs = (P("dep", None, "lat"), P(None, "lat"), P(), P("dep", None, "lat"))
    out_specs = (P("dep", None, "lat"), P())
    return jax.shard_map(per_device, mesh=mesh, in_specs=in_specs, out_specs=out_specs, check_vma=False)
```

```python
import math

import jax
import jax.numpy as jnp
from jax import lax
from jax.experimental import pallas as pl
from jax.experimental.pallas import tpu as pltpu
from jax.sharding import PartitionSpec as P


NZONE = 16
CP, CF, CF2, CB, CL, UNROLL = 48, 48, 40, 40, 32, False
CORE = 32
HALO = 8
WIDE = CORE + 2 * HALO
SEED_HALO = 4
SEED_WIDE = CORE + 2 * SEED_HALO
BASE = 8
HIGH = WIDE + 2 * BASE
DT = 0.1
ABSORB_SOLID = 0.004
ABSORB_RISE = 0.026
LOG2E = math.log2(math.e)
EM10 = math.exp(-10.0)
F32 = jnp.float32


def _params():
    return pltpu.CompilerParams(vmem_limit_bytes=16 * 1024 * 1024)


def _vmem(*shape):
    return pltpu.VMEM(shape, F32)


def _full():
    return pl.BlockSpec(memory_space=pltpu.VMEM)


def _any():
    return pl.BlockSpec(memory_space=pltpu.HBM)


def _lanes(rows=8):
    return lax.broadcasted_iota(jnp.int32, (rows, 128), 1)


def _chunks(count, size, unrolled, body):
    if count == size:
        body(0)
    elif unrolled:
        for c in range(count // size):
            body(c)
    else:
        lax.fori_loop(0, count // size, lambda c, carry: (body(c), carry)[1], 0)


def _packed(ref, g, d):
    tiles = []
    for p in range(4):
        rf = lax.rem(p + 4 - d, 4)
        tiles += [ref[8 * sub + g, pl.ds(rf, 8, stride=4)] for sub in range(4)]
    return jnp.concatenate(tiles, axis=0).T


def _surface(ref, rf):
    return jnp.concatenate([ref[pl.ds(rf, 8, stride=4)]] * 16, axis=0).T


def pack(fluence_in, h_in, zones_in, a_in, state, seed, light, zid, to_inner, to_outer, edges, h, a, zones, flat, zbuf, fluence, sems):
    d = lax.axis_index("dep")
    to_left, to_right = edges.at[0], edges.at[1]
    copies = [
        pltpu.make_async_copy(source, target, sems.at[k])
        for k, (source, target) in enumerate(((h_in, h), (zones_in, zones), (fluence_in, fluence), (a_in, a)))
    ]
    for copy in copies:
        copy.start()
    copies[0].wait()
    for g in range(8):
        packed = _packed(h, g, d)
        state[g] = packed
        to_left[g, 0:8] = packed[0:8]
        to_right[g, 0:8] = packed[120:128]
    copies[1].wait()
    copies[2].wait()
    ids = zones[...]
    intensity = jnp.zeros(ids.shape, F32)
    for k in range(NZONE):
        intensity = jnp.where(ids == k, fluence[k] * DT, intensity)
    flat[0] = intensity
    flat[1] = ids.astype(F32)
    start = pl.multiple_of(d * CORE, CORE)
    for rf in range(4):
        packed = _surface(flat.at[0], rf)
        light[rf] = packed
        for half in range(2):
            to_left[2 * rf + half, 12:16] = packed[4 * half : 4 * half + 4]
            to_right[2 * rf + half, 12:16] = packed[120 + 4 * half : 124 + 4 * half]
        zbuf[...] = _surface(flat.at[1], rf)
        zid[rf] = zbuf[pl.ds(start, CORE)]
    copies[3].wait()
    for g in range(8):
        packed = _packed(a, g, d)
        seed[g] = packed
        to_left[g, 8:12] = packed[0:4]
        to_right[g, 8:12] = packed[124:128]
    odd = lax.rem(lax.axis_index("lat"), 2)
    to_inner[...] = edges[1 - odd]
    to_outer[...] = edges[odd]


def insert(state, seed, light, inner, outer, h0, h1, h2, h3, s0, s1, s2, s3, light_own, sides, hbuf, sbuf, lbuf):
    odd = lax.rem(lax.axis_index("lat"), 2)
    sides[odd] = outer[...]
    sides[1 - odd] = inner[...]
    right, left = sides.at[1], sides.at[0]
    d = lax.axis_index("dep")
    hbuf[:, 0:8] = left[:, 0:8]
    hbuf[:, 8:136] = state[...]
    hbuf[:, 136:144] = right[:, 0:8]
    for k, out in enumerate((h0, h1, h2, h3)):
        start = pl.multiple_of(lax.rem(d + k, 4) * CORE, CORE)
        out[...] = hbuf[:, pl.ds(start, WIDE)]
    sbuf[:, 0:4] = left[:, 8:12]
    sbuf[:, 4:132] = seed[...]
    sbuf[:, 132:136] = right[:, 8:12]
    for k, out in enumerate((s0, s1, s2, s3)):
        start = pl.multiple_of(lax.rem(d + k, 4) * CORE, CORE)
        out[...] = sbuf[:, pl.ds(start, SEED_WIDE)]
    start = pl.multiple_of(d * CORE, CORE)
    for rf in range(4):
        for half in range(2):
            lbuf[4 * half : 4 * half + 4] = left[2 * rf + half, 12:16]
            lbuf[136 + 4 * half : 140 + 4 * half] = right[2 * rf + half, 12:16]
        lbuf[8:136] = light[rf]
        light_own[rf] = lbuf[pl.ds(start, WIDE)]


def _source_masks():
    part = lax.rem(_lanes(8) // 32 + 4 - lax.axis_index("dep"), 4)
    return [part == j for j in range(4)]


def _pick(masks, shift, values):
    return jnp.where(
        masks[shift % 4],
        values[0],
        jnp.where(masks[(shift + 1) % 4], values[1], jnp.where(masks[(shift + 2) % 4], values[2], values[3])),
    )


def _gather(blocks, field, first, count):
    masks = _source_masks()

    def tile(i, carry):
        g, c = i // (count // 8), pl.multiple_of(lax.rem(i, count // 8) * 8, 8)
        own, r1, r2, r3 = [block[g, pl.ds(c, 8)] for block in blocks]
        for rf in range(4):
            mixed = _pick(masks, rf, (own, r3, r2, r1))
            field[8 * rf + g, pl.ds(BASE + first + c, 8)] = mixed if rf == 0 else pltpu.roll(mixed, 128 - 32 * rf, 1)
        return carry

    lax.fori_loop(0, count, tile, 0, unroll=2)


class _Tiles:
    def __init__(self, row, rows):
        self.rows = rows
        self.here, self.up, self.down = pl.ds(row, rows), pl.ds(row + 1, rows), pl.ds(row - 1, rows)


def _inclusive(total, lane, reverse):
    for step in (8, 16, 32, 64):
        if reverse:
            total = total + jnp.where(lane < 128 - step, pltpu.roll(total, 128 - step, 1), 0.0)
        else:
            total = total + jnp.where(lane >= step, pltpu.roll(total, step, 1), 0.0)
    return total


def _properties(n, rf, tiles, states, t_ref, k_ref, c_ref, r_ref, l_ref):
    lane = _lanes(tiles.rows)
    here = tiles.here
    run = jnp.zeros((tiles.rows, 128), F32)
    runs = []
    for g in range(8):
        i = 8 * rf + g
        h = states[g]
        e = jnp.exp2(h * (10.0 * LOG2E) - 10.0 * LOG2E)
        u = 1.0 + e
        v = 1.0 + EM10 * e
        inv = pl.reciprocal(u * v)
        ramp = 0.1 * jnp.log(u * (u * inv))
        t = h - ramp
        m = pl.reciprocal(1.0 + t * t)
        t_ref[n, i, here] = t
        k_ref[n, i, here] = 0.03 + 0.04 * m
        c_ref[n, i, here] = (-0.08 * t) * (m * m)
        r_ref[n, i, here] = e * ((1.0 - EM10) * inv)
        runs.append(run)
        run = run + (ABSORB_SOLID * LOG2E + (ABSORB_RISE * LOG2E) * ramp)
    above = _inclusive(run, lane, False) - run
    for g in range(8):
        l_ref[n, 9 * rf + g, here] = jnp.exp2(-(above + runs[g]))
    l_ref[n, 9 * rf + 8, here] = jnp.exp2(-(above + run))


def _advance(n, tiles, h_ref, t_ref, k_ref, l_ref, light, then):
    lane = _lanes(tiles.rows)
    inside = lax.rem(lane, 8) < 7
    above_bottom = lane < 120
    here, up, down = tiles.here, tiles.up, tiles.down

    def across(g):
        t3, k3 = t_ref[n, 24 + g, here], k_ref[n, 24 + g, here]
        t0, k0 = pltpu.roll(t_ref[n, g, here], 127, 1), pltpu.roll(k_ref[n, g, here], 127, 1)
        return jnp.where(inside, (k3 + k0) * (t0 - t3), 0.0)

    last = [across(g) for g in range(8)]
    before = [pltpu.roll(f, 1, 1) for f in last]
    for rf in range(4):
        i0 = 8 * rf
        t = [t_ref[n, i0 + g, here] for g in range(8)]
        k = [k_ref[n, i0 + g, here] for g in range(8)]
        end = jnp.where(above_bottom, (k[7] + pltpu.roll(k[0], 120, 1)) * (pltpu.roll(t[0], 120, 1) - t[7]), 0.0)
        flux_before = pltpu.roll(end, 8, 1)
        new = []
        for g in range(8):
            i = i0 + g
            if g < 7:
                flux = (k[g] + k[g + 1]) * (t[g + 1] - t[g])
            else:
                flux = jnp.where(above_bottom, end, -0.05 * t[7])
            if rf < 3:
                side = (k[g] + k_ref[n, i + 8, here]) * (t_ref[n, i + 8, here] - t[g])
            else:
                side = last[g]
            change = (flux - flux_before) + (side - before[g])
            change = change + (
                (k[g] + k_ref[n, i, up]) * (t_ref[n, i, up] - t[g])
                - (k[g] + k_ref[n, i, down]) * (t[g] - t_ref[n, i, down])
            )
            source = light[rf, here] * (l_ref[n, 9 * rf + g, here] - l_ref[n, 9 * rf + g + 1, here])
            new.append(h_ref[i, here] + (change + source))
            flux_before, before[g] = flux, side
        then(rf, new)


def _ghost(ref_rows):
    lat, d = lax.axis_index("lat"), lax.axis_index("dep")

    @pl.when(jnp.logical_and(lat == 0, d == 0))
    def _():
        for i in range(32):
            ref_rows(i, HALO - 1)[...] = ref_rows(i, HALO)[...]

    @pl.when(jnp.logical_and(lat == 31, d == 3))
    def _():
        for i in range(32):
            ref_rows(i, HALO + CORE)[...] = ref_rows(i, HALO + CORE - 1)[...]


def forward(own, r1, r2, r3, light_own, t_ref, k_ref, c_ref, r_ref, l_ref, light, ha, hb):
    _gather((own, r1, r2, r3), ha, 0, WIDE)
    for rf in range(4):
        light[rf, BASE : BASE + WIDE] = light_own[rf]
    fields = (t_ref, k_ref, c_ref, r_ref, l_ref)

    def start(c):
        tiles = _Tiles(BASE + CP * c, CP)
        for rf in range(4):
            _properties(0, rf, tiles, [ha[8 * rf + g, tiles.here] for g in range(8)], *fields)

    _chunks(WIDE, CP, UNROLL, start)
    source, target = ha, hb
    for n in range(3):
        _ghost(lambda i, c, n=n: t_ref.at[n, i, pl.ds(BASE + c, 1)])
        first, count = (0, WIDE) if n < 2 else (SEED_HALO, SEED_WIDE)

        size = CF if n < 2 else CF2

        def chunk(c, n=n, first=first, source=source, target=target, size=size):
            tiles = _Tiles(BASE + first + size * c, size)

            def then(rf, new):
                for g in range(8):
                    if n < 2:
                        target[8 * rf + g, tiles.here] = new[g]
                _properties(n + 1, rf, tiles, new, *fields)

            _advance(n, tiles, source, t_ref, k_ref, l_ref, light, then)

        _chunks(count, size, UNROLL, chunk)
        source, target = target, source


def _retreat(n, tiles, a_ref, t_ref, k_ref, c_ref, r_ref, l_ref, light, put, seen):
    lane = _lanes(tiles.rows)
    inside = lax.rem(lane, 8) < 7
    above_bottom = lane < 120
    here, up, down = tiles.here, tiles.up, tiles.down

    def across(g):
        a3, t3, k3 = a_ref[24 + g, here], t_ref[n, 24 + g, here], k_ref[n, 24 + g, here]
        a0, t0, k0 = [pltpu.roll(x, 127, 1) for x in (a_ref[g, here], t_ref[n, g, here], k_ref[n, g, here])]
        jump = jnp.where(inside, a3 - a0, 0.0)
        return jump * (k3 + k0), jump * (t0 - t3)

    last = [across(g) for g in range(8)]
    before = [(pltpu.roll(push, 1, 1), pltpu.roll(share, 1, 1)) for push, share in last]
    for rf in range(4):
        i0 = 8 * rf
        a = [a_ref[i0 + g, here] for g in range(8)]
        t = [t_ref[n, i0 + g, here] for g in range(8)]
        k = [k_ref[n, i0 + g, here] for g in range(8)]
        run = jnp.zeros((tiles.rows, 128), F32)
        runs = [None] * 8
        for g in reversed(range(8)):
            runs[g] = run
            run = run + a[g] * (l_ref[n, 9 * rf + g, here] - l_ref[n, 9 * rf + g + 1, here])
        below = _inclusive(run, lane, True) - run
        seen(rf, run)
        gain = ABSORB_RISE * light[rf, here]
        jump = jnp.where(above_bottom, a[7] - pltpu.roll(a[0], 120, 1), 0.0)
        push_end = jump * (k[7] + pltpu.roll(k[0], 120, 1))
        share_end = jump * (pltpu.roll(t[0], 120, 1) - t[7])
        push_before, share_before = pltpu.roll(push_end, 8, 1), pltpu.roll(share_end, 8, 1)
        for g in range(8):
            i = i0 + g
            if g < 7:
                jump = a[g] - a[g + 1]
                push, share = jump * (k[g] + k[g + 1]), jump * (t[g + 1] - t[g])
            else:
                push, share = jnp.where(above_bottom, push_end, 0.05 * a[7]), share_end
            if rf < 3:
                jump = a[g] - a_ref[i + 8, here]
                push_r, share_r = jump * (k[g] + k_ref[n, i + 8, here]), jump * (t_ref[n, i + 8, here] - t[g])
            else:
                push_r, share_r = last[g]
            grad_t = (push_before - push) + (before[g][0] - push_r)
            grad_k = (share_before + share) + (before[g][1] + share_r)
            jump_up = a[g] - a_ref[i, up]
            jump_down = a_ref[i, down] - a[g]
            grad_t = grad_t + (jump_down * (k_ref[n, i, down] + k[g]) - jump_up * (k[g] + k_ref[n, i, up]))
            grad_k = grad_k + (jump_down * (t[g] - t_ref[n, i, down]) + jump_up * (t_ref[n, i, up] - t[g]))
            heat = grad_t + c_ref[n, i, here] * grad_k
            absorbed = gain * (a[g] * l_ref[n, 9 * rf + g + 1, here] - (below + runs[g]))
            put(i, a[g] + (heat + r_ref[n, i, here] * (absorbed - heat)))
            push_before, share_before, before[g] = push, share, (push_r, share_r)


def backward(own, r1, r2, r3, t_ref, k_ref, c_ref, r_ref, l_ref, light, zid, a_ref, zpart, ab, total):
    _gather((own, r1, r2, r3), ab, SEED_HALO, SEED_WIDE)
    fields = (t_ref, k_ref, c_ref, r_ref, l_ref, light)
    total[...] = jnp.zeros(total.shape, F32)
    source, target = ab, a_ref
    for n in (3, 2, 1):
        _ghost(lambda i, c, ref=source: ref.at[i, pl.ds(BASE + c, 1)])

        def chunk(c, n=n, source=source, target=target):
            tiles = _Tiles(BASE + SEED_HALO + CB * c, CB)

            def put(i, value):
                target[i, tiles.here] = value

            def seen(rf, value):
                total[rf, tiles.here] += value

            _retreat(n, tiles, source, *fields, put, seen)

        _chunks(SEED_WIDE, CB, UNROLL, chunk)
        source, target = target, source
    _ghost(lambda i, c, ref=source: ref.at[i, pl.ds(BASE + c, 1)])
    core = pl.ds(BASE + HALO, CORE)
    sums = []
    for rf in range(4):
        value = total[rf, core]
        for g in range(8):
            value = value + source[8 * rf + g, core] * (l_ref[0, 9 * rf + g, core] - l_ref[0, 9 * rf + g + 1, core])
        sums.append(value * DT)
    rows = []
    for z in range(NZONE):
        picked = [jnp.where(zid[rf] == float(z), sums[rf], 0.0) for rf in range(4)]
        rows.append(jnp.sum((picked[0] + picked[1]) + (picked[2] + picked[3]), axis=0, keepdims=True))
    spread = jnp.concatenate(rows + [jnp.zeros((128 - NZONE, 128), F32)], axis=0)
    zpart[...] = jnp.sum(spread.T, axis=0, keepdims=True)


def last_step(a_ref, t_ref, k_ref, c_ref, r_ref, l_ref, light, o0, o1, o2, o3):
    masks = [jnp.broadcast_to(m[0:1], (CL, 128)) for m in _source_masks()]

    def chunk(c):
        tiles = _Tiles(BASE + HALO + CL * c, CL)
        values = [None] * 32

        def put(i, value):
            values[i] = value

        _retreat(0, tiles, a_ref, t_ref, k_ref, c_ref, r_ref, l_ref, light, put, lambda rf, value: None)
        for g in range(8):
            turned = [values[g]] + [pltpu.roll(values[8 * rf + g], 32 * rf, 1) for rf in (1, 2, 3)]
            for k, out in enumerate((o0, o1, o2, o3)):
                out[g, pl.ds(pl.multiple_of(CL * c, 8), CL)] = _pick(masks, k, turned)

    _chunks(CORE, CL, UNROLL, chunk)


def unpack(own, r1, r2, r3, parts, out, total, buf):
    d = lax.axis_index("dep")
    for k, block in enumerate((own, r1, r2, r3)):
        start = pl.multiple_of(lax.rem(d + 4 - k, 4) * CORE, CORE)
        buf[:, pl.ds(start, CORE)] = block[...]
    for g in range(8):
        plain = buf[g].T
        for p in range(4):
            rf = lax.rem(p + 4 - d, 4)
            for sub in range(4):
                out[8 * sub + g, pl.ds(rf, 8, stride=4)] = plain[32 * p + 8 * sub : 32 * p + 8 * sub + 8]
    total[...] = jnp.sum(parts[...], axis=0)


def _around(x, k):
    return lax.ppermute(x, "dep", [(s, (s + k) % 4) for s in range(4)])


def _place(y, z, core, x):
    return ((y * 4 + z) * 2 + core) * 4 + x


def _meet(v, partner):
    pairs = []
    for y in range(4):
        for z in range(4):
            for core in range(2):
                for x in range(4):
                    pairs.append((_place(y, z, core, x), _place(*partner(y, z, core, x))))
    return v + lax.ppermute(v, ("lat", "dep"), pairs)


def _shape(*dims):
    return jax.ShapeDtypeStruct(dims, F32)


def _call(kernel, inputs, outs, scratch=(), spaces=None):
    return pl.pallas_call(
        kernel,
        out_shape=tuple(outs),
        in_specs=spaces or [_full()] * len(inputs),
        out_specs=(_full(),) * len(outs),
        scratch_shapes=list(scratch),
        compiler_params=_params(),
        name=kernel.__name__,
    )(*inputs)


def per_device(h, zones, fluence, seed):
    slab = _shape(8, 128, 128)
    edge = _shape(8, 16, 128)
    state, start, light, zid, to_inner, to_outer = _call(
        pack,
        tuple(pltpu.with_memory_space_constraint(x, pltpu.HBM) for x in (fluence, h, zones, seed)),
        (slab, slab, _shape(4, 128, 128), _shape(4, CORE, 128), edge, edge),
        (
            _vmem(2, 8, 16, 128),
            _vmem(32, 32, 128),
            _vmem(32, 32, 128),
            pltpu.VMEM((32, 128), jnp.int32),
            _vmem(2, 32, 128),
            _vmem(128, 128),
            pltpu.SMEM((NZONE,), F32),
            pltpu.SemaphoreType.DMA((4,)),
        ),
        [_any()] * 4,
    )
    outer = lax.ppermute(to_outer, "lat", [pair for l in range(1, 31, 2) for pair in ((l, l + 1), (l + 1, l))])
    inner = lax.ppermute(to_inner, "lat", [pair for l in range(0, 32, 2) for pair in ((l, l + 1), (l + 1, l))])
    block, seed_block = _shape(8, WIDE, 128), _shape(8, SEED_WIDE, 128)
    h0, h1, h2, h3, s0, s1, s2, s3, light_own = _call(
        insert,
        (state, start, light, inner, outer),
        (block,) * 4 + (seed_block,) * 4 + (_shape(4, WIDE, 128),),
        (_vmem(2, 8, 16, 128), _vmem(8, 144, 128), _vmem(8, 136, 128), _vmem(144, 128)),
    )
    h2, h1, h3 = _around(h2, 2), _around(h1, 1), _around(h3, 3)
    s2, s1, s3 = _around(s2, 2), _around(s1, 1), _around(s3, 3)
    field = _vmem(4, 32, HIGH, 128)
    states = _call(
        forward,
        (h0, h1, h2, h3, light_own),
        (field,) * 4 + (_vmem(4, 36, HIGH, 128), _vmem(4, HIGH, 128)),
        [_vmem(32, HIGH, 128)] * 2,
    )
    a, zpart = _call(
        backward,
        (s0, s1, s2, s3, *states, zid),
        (_vmem(32, HIGH, 128), _shape(1, 128)),
        (_vmem(32, HIGH, 128), _vmem(4, HIGH, 128)),
    )
    piece = _shape(8, CORE, 128)
    o0, o1, o2, o3 = _call(last_step, (a, *states), (piece,) * 4)
    o2, o1, o3 = _around(o2, 2), _around(o1, 1), _around(o3, 3)
    parts = lax.all_to_all(jnp.broadcast_to(zpart[None], (128, 1, 128)), ("lat", "dep"), 0, 0)
    out, total = _call(unpack, (o0, o1, o2, o3, parts), (_shape(32, 32, 128), _shape(1, 128)), (_vmem(8, 128, 128),))
    total = total[0, :NZONE]
    return out, total


def solution(mesh):
    in_specs = (P("dep", None, "lat"), P(None, "lat"), P(), P("dep", None, "lat"))
    out_specs = (P("dep", None, "lat"), P())
    return jax.shard_map(per_device, mesh=mesh, in_specs=in_specs, out_specs=out_specs, check_vma=False)
```

```python
import math

import jax
import jax.numpy as jnp
from jax import lax
from jax.experimental import pallas as pl
from jax.experimental.pallas import tpu as pltpu
from jax.sharding import PartitionSpec as P


NZONE = 16
CORE = 32
HALO = 8
WIDE = CORE + 2 * HALO
SEED_HALO = 4
SEED_WIDE = CORE + 2 * SEED_HALO
BASE = 8
HIGH = WIDE + 2 * BASE
DT = 0.1
ABSORB_SOLID = 0.004
ABSORB_RISE = 0.026
LOG2E = math.log2(math.e)
EM10 = math.exp(-10.0)
F32 = jnp.float32


def _params():
    return pltpu.CompilerParams(vmem_limit_bytes=16 * 1024 * 1024)


def _group(d):
    return jnp.where(lax.rem(lax.axis_index("lat"), 2) == 0, d, 3 - d)


def _columns(d):
    return pl.ds(pl.multiple_of(_group(d) * CORE, CORE), CORE)


def _vmem(*shape):
    return pltpu.VMEM(shape, F32)


def _full():
    return pl.BlockSpec(memory_space=pltpu.VMEM)


def _lanes(rows=8):
    return lax.broadcasted_iota(jnp.int32, (rows, 128), 1)


def _packed(ref, g, d):
    tiles = []
    for p in range(4):
        rf = lax.rem(p + 4 - d, 4)
        tiles += [ref[8 * sub + g, pl.ds(rf, 8, stride=4)] for sub in range(4)]
    return jnp.concatenate(tiles, axis=0).T


def _surface(ref, rf):
    return jnp.concatenate([ref[pl.ds(rf, 8, stride=4)]] * 16, axis=0).T


def pack_state(h_in, h0, h1, h2, h3, h, buf, sem):
    d = lax.axis_index("dep")
    copy = pltpu.make_async_copy(h_in, h, sem)
    copy.start()
    copy.wait()
    for g in range(8):
        buf[g] = _packed(h, g, d)
    for k, out in enumerate((h0, h1, h2, h3)):
        out[...] = buf[:, _columns(lax.rem(d + k, 4))]


def pack_rest(fluence_in, zones_in, a_in, seed, light, zid, to_inner, to_outer, edges, a, zones, flat, zbuf, fluence, sems):
    d = lax.axis_index("dep")
    to_left, to_right = edges.at[0], edges.at[1]
    copies = [
        pltpu.make_async_copy(source, target, sems.at[k])
        for k, (source, target) in enumerate(((fluence_in, fluence), (zones_in, zones), (a_in, a)))
    ]
    for copy in copies:
        copy.start()
    copies[0].wait()
    copies[1].wait()
    ids = zones[...]
    intensity = jnp.zeros(ids.shape, F32)
    for k in range(NZONE):
        intensity = jnp.where(ids == k, fluence[k] * DT, intensity)
    flat[0] = intensity
    flat[1] = ids.astype(F32)
    for rf in range(4):
        packed = _surface(flat.at[0], rf)
        light[rf] = packed
        for half in range(2):
            to_left[2 * rf + half, 4:8] = packed[4 * half : 4 * half + 4]
            to_right[2 * rf + half, 4:8] = packed[120 + 4 * half : 124 + 4 * half]
        zbuf[...] = _surface(flat.at[1], rf)
        zid[rf] = zbuf[_columns(d)]
    copies[2].wait()
    for g in range(8):
        packed = _packed(a, g, d)
        seed[g] = packed
        to_left[g, 0:4] = packed[0:4]
        to_right[g, 0:4] = packed[124:128]
    odd = lax.rem(lax.axis_index("lat"), 2)
    to_inner[...] = edges[1 - odd]
    to_outer[...] = edges[odd]


def insert(seed, light, inner, outer, s0, s1, s2, s3, light_own, sides, sbuf, lbuf):
    d = lax.axis_index("dep")
    odd = lax.rem(lax.axis_index("lat"), 2)
    sides[odd] = outer[...]
    sides[1 - odd] = inner[...]
    left, right = sides.at[0], sides.at[1]
    sbuf[:, 0:4] = left[:, 0:4]
    sbuf[:, 4:132] = seed[...]
    sbuf[:, 132:136] = right[:, 0:4]
    for k, out in enumerate((s0, s1, s2, s3)):
        start = pl.multiple_of(_group(lax.rem(d + k, 4)) * CORE, CORE)
        out[...] = sbuf[:, pl.ds(start, SEED_WIDE)]
    start = pl.multiple_of(_group(d) * CORE, CORE)
    for rf in range(4):
        for half in range(2):
            lbuf[4 * half : 4 * half + 4] = left[2 * rf + half, 4:8]
            lbuf[136 + 4 * half : 140 + 4 * half] = right[2 * rf + half, 4:8]
        lbuf[8:136] = light[rf]
        light_own[rf, 0:BASE] = jnp.zeros((BASE, 128), F32)
        light_own[rf, BASE : BASE + WIDE] = lbuf[pl.ds(start, WIDE)]
        light_own[rf, BASE + WIDE :] = jnp.zeros((BASE, 128), F32)


def _source_masks():
    part = lax.rem(_lanes(8) // 32 + 4 - lax.axis_index("dep"), 4)
    return [part == j for j in range(4)]


def _pick(masks, shift, values):
    return jnp.where(
        masks[shift % 4],
        values[0],
        jnp.where(masks[(shift + 1) % 4], values[1], jnp.where(masks[(shift + 2) % 4], values[2], values[3])),
    )


def _gather(blocks, field, first, count):
    masks = [jnp.broadcast_to(m[0:1], (count, 128)) for m in _source_masks()]
    for g in range(8):
        own, r1, r2, r3 = [block[g] for block in blocks]
        for rf in range(4):
            mixed = _pick(masks, rf, (own, r3, r2, r1))
            field[8 * rf + g, pl.ds(BASE + first, count)] = mixed if rf == 0 else pltpu.roll(mixed, 128 - 32 * rf, 1)


class _Tiles:
    def __init__(self, row, rows, exact):
        self.rows, self.exact = rows, exact
        self.here, self.up, self.down = pl.ds(row, rows), pl.ds(row + 1, rows), pl.ds(row - 1, rows)


def _inclusive(total, lane, reverse):
    a = lax.broadcasted_iota(jnp.int32, (128, 128), 0)
    b = lax.broadcasted_iota(jnp.int32, (128, 128), 1)
    same = lax.rem(a, 8) == lax.rem(b, 8)
    tri = jnp.where(jnp.logical_and(same, a >= b if reverse else a <= b), 1.0, 0.0).astype(jnp.bfloat16)
    high = total.astype(jnp.bfloat16)
    low = (total - high.astype(F32)).astype(jnp.bfloat16)
    return jnp.dot(high, tri, preferred_element_type=F32) + jnp.dot(low, tri, preferred_element_type=F32)


def _properties(n, rf, tiles, states, t_ref, k_ref, c_ref, r_ref, l_ref):
    lane = _lanes(tiles.rows)
    here = tiles.here
    run = jnp.zeros((tiles.rows, 128), F32)
    runs = []
    for g in range(8):
        i = 8 * rf + g
        h = states[g]
        e = jnp.exp2(h * (10.0 * LOG2E) - 10.0 * LOG2E)
        u = 1.0 + e
        v = 1.0 + EM10 * e
        inv = pl.reciprocal(u * v)
        ramp = 0.1 * jnp.log(u * (u * inv))
        t = h - ramp
        m = pl.reciprocal(1.0 + t * t)
        t_ref[n, i, here] = t
        k_ref[n, i, here] = 0.03 + 0.04 * m
        c_ref[n, i, here] = (-0.08 * t) * (m * m)
        r_ref[n, i, here] = e * ((1.0 - EM10) * inv)
        runs.append(run)
        run = run + (ABSORB_SOLID * LOG2E + (ABSORB_RISE * LOG2E) * ramp)
    above = _inclusive(run, lane, False) - run
    for g in range(8):
        l_ref[n, 9 * rf + g, here] = jnp.exp2(-(above + runs[g]))
    l_ref[n, 9 * rf + 8, here] = jnp.exp2(-(above + run))


def _advance(n, tiles, h_ref, t_ref, k_ref, l_ref, light, then):
    lane = _lanes(tiles.rows)
    inside = lax.rem(lane, 8) < 7
    above_bottom = lane < 120
    here, up, down = tiles.here, tiles.up, tiles.down

    def across(g):
        t3, k3 = t_ref[n, 24 + g, here], k_ref[n, 24 + g, here]
        t0, k0 = pltpu.roll(t_ref[n, g, here], 127, 1), pltpu.roll(k_ref[n, g, here], 127, 1)
        return jnp.where(inside, (k3 + k0) * (t0 - t3), 0.0)

    last = [across(g) for g in range(8)]
    before = [pltpu.roll(f, 1, 1) for f in last]
    for rf in range(4):
        i0 = 8 * rf
        t = [t_ref[n, i0 + g, here] for g in range(8)]
        k = [k_ref[n, i0 + g, here] for g in range(8)]
        end = jnp.where(above_bottom, (k[7] + pltpu.roll(k[0], 120, 1)) * (pltpu.roll(t[0], 120, 1) - t[7]), 0.0)
        flux_before = pltpu.roll(end, 8, 1)
        new = []
        for g in range(8):
            i = i0 + g
            if g < 7:
                flux = (k[g] + k[g + 1]) * (t[g + 1] - t[g])
            else:
                flux = jnp.where(above_bottom, end, -0.05 * t[7])
            if rf < 3:
                side = (k[g] + k_ref[n, i + 8, here]) * (t_ref[n, i + 8, here] - t[g])
            else:
                side = last[g]
            change = (flux - flux_before) + (side - before[g])
            col = (k[g] + k_ref[n, i, up]) * (t_ref[n, i, up] - t[g])
            if tiles.exact:
                col_before = (k_ref[n, i, down] + k[g]) * (t[g] - t_ref[n, i, down])
            else:
                col_before = pltpu.roll(col, 1, 0)
            change = change + (col - col_before)
            source = light[rf, here] * (l_ref[n, 9 * rf + g, here] - l_ref[n, 9 * rf + g + 1, here])
            new.append(h_ref[i, here] + (change + source))
            flux_before, before[g] = flux, side
        then(rf, new)


def _ghost(ref_rows):
    lat, group = lax.axis_index("lat"), _group(lax.axis_index("dep"))

    @pl.when(jnp.logical_and(lat == 0, group == 0))
    def _():
        for i in range(32):
            ref_rows(i, HALO - 1)[...] = ref_rows(i, HALO)[...]

    @pl.when(jnp.logical_and(lat == 31, group == 3))
    def _():
        for i in range(32):
            ref_rows(i, HALO + CORE)[...] = ref_rows(i, HALO + CORE - 1)[...]


def gather_state(own, r1, r2, r3, h0, to_inner, to_outer):
    _gather((own, r1, r2, r3), h0, HALO, CORE)
    odd = lax.rem(_group(lax.axis_index("dep")), 2)
    first, last = BASE + HALO, BASE + CORE
    to_inner[...] = h0[:, pl.ds(pl.multiple_of(jnp.where(odd == 1, first, last), 8), HALO)]
    to_outer[...] = h0[:, pl.ds(pl.multiple_of(jnp.where(odd == 1, last, first), 8), HALO)]


def forward_core(h0, light, h1, h2, t_ref, k_ref, c_ref, r_ref, l_ref):
    fields = (t_ref, k_ref, c_ref, r_ref, l_ref)
    tiles = _Tiles(BASE + HALO, CORE, False)
    for rf in range(4):
        _properties(0, rf, tiles, [h0[8 * rf + g, tiles.here] for g in range(8)], *fields)
    for n, source, target in ((0, h0, h1), (1, h1, h2), (2, h2, None)):

        def then(rf, new, n=n, target=target):
            if target is not None:
                for g in range(8):
                    target[8 * rf + g, tiles.here] = new[g]
            _properties(n + 1, rf, tiles, new, *fields)

        _advance(n, tiles, source, t_ref, k_ref, l_ref, light, then)


def forward_sides(inner, outer, light, *refs):
    h0, h1, h2, t_ref, k_ref, c_ref, r_ref, l_ref = refs[8:]
    fields = (t_ref, k_ref, c_ref, r_ref, l_ref)
    even = lax.rem(_group(lax.axis_index("dep")), 2) == 0

    @pl.when(even)
    def _():
        h0[:, BASE : BASE + HALO] = outer[...]
        h0[:, BASE + HALO + CORE : BASE + WIDE] = inner[...]

    @pl.when(jnp.logical_not(even))
    def _():
        h0[:, BASE : BASE + HALO] = inner[...]
        h0[:, BASE + HALO + CORE : BASE + WIDE] = outer[...]

    for first in (0, HALO + CORE):
        tiles = _Tiles(BASE + first, HALO, False)
        for rf in range(4):
            _properties(0, rf, tiles, [h0[8 * rf + g, tiles.here] for g in range(8)], *fields)
    for n, source, target in ((0, h0, h1), (1, h1, h2), (2, h2, None)):
        _ghost(lambda i, c, n=n: t_ref.at[n, i, pl.ds(BASE + c, 1)])
        for first in (n + 1, HALO + CORE - 1 - n):
            tiles = _Tiles(BASE + first, HALO, True)

            def then(rf, new, n=n, target=target, tiles=tiles):
                if target is not None:
                    for g in range(8):
                        target[8 * rf + g, tiles.here] = new[g]
                _properties(n + 1, rf, tiles, new, *fields)

            _advance(n, tiles, source, t_ref, k_ref, l_ref, light, then)


def _retreat(n, tiles, a_ref, t_ref, k_ref, c_ref, r_ref, l_ref, light, put, seen):
    lane = _lanes(tiles.rows)
    inside = lax.rem(lane, 8) < 7
    above_bottom = lane < 120
    here, up, down = tiles.here, tiles.up, tiles.down

    def across(g):
        a3, t3, k3 = a_ref[24 + g, here], t_ref[n, 24 + g, here], k_ref[n, 24 + g, here]
        a0, t0, k0 = [pltpu.roll(x, 127, 1) for x in (a_ref[g, here], t_ref[n, g, here], k_ref[n, g, here])]
        jump = jnp.where(inside, a3 - a0, 0.0)
        return jump * (k3 + k0), jump * (t0 - t3)

    last = [across(g) for g in range(8)]
    before = [(pltpu.roll(push, 1, 1), pltpu.roll(share, 1, 1)) for push, share in last]
    for rf in range(4):
        i0 = 8 * rf
        a = [a_ref[i0 + g, here] for g in range(8)]
        t = [t_ref[n, i0 + g, here] for g in range(8)]
        k = [k_ref[n, i0 + g, here] for g in range(8)]
        run = jnp.zeros((tiles.rows, 128), F32)
        runs = [None] * 8
        for g in reversed(range(8)):
            runs[g] = run
            run = run + a[g] * (l_ref[n, 9 * rf + g, here] - l_ref[n, 9 * rf + g + 1, here])
        below = _inclusive(run, lane, True) - run
        seen(rf, run)
        gain = ABSORB_RISE * light[rf, here]
        jump = jnp.where(above_bottom, a[7] - pltpu.roll(a[0], 120, 1), 0.0)
        push_end = jump * (k[7] + pltpu.roll(k[0], 120, 1))
        share_end = jump * (pltpu.roll(t[0], 120, 1) - t[7])
        push_before, share_before = pltpu.roll(push_end, 8, 1), pltpu.roll(share_end, 8, 1)
        for g in range(8):
            i = i0 + g
            if g < 7:
                jump = a[g] - a[g + 1]
                push, share = jump * (k[g] + k[g + 1]), jump * (t[g + 1] - t[g])
            else:
                push, share = jnp.where(above_bottom, push_end, 0.05 * a[7]), share_end
            if rf < 3:
                jump = a[g] - a_ref[i + 8, here]
                push_r, share_r = jump * (k[g] + k_ref[n, i + 8, here]), jump * (t_ref[n, i + 8, here] - t[g])
            else:
                push_r, share_r = last[g]
            grad_t = (push_before - push) + (before[g][0] - push_r)
            grad_k = (share_before + share) + (before[g][1] + share_r)
            jump = a[g] - a_ref[i, up]
            push_c, share_c = jump * (k[g] + k_ref[n, i, up]), jump * (t_ref[n, i, up] - t[g])
            if tiles.exact:
                jump = a_ref[i, down] - a[g]
                push_d, share_d = jump * (k_ref[n, i, down] + k[g]), jump * (t[g] - t_ref[n, i, down])
            else:
                push_d, share_d = pltpu.roll(push_c, 1, 0), pltpu.roll(share_c, 1, 0)
            grad_t = grad_t + (push_d - push_c)
            grad_k = grad_k + (share_d + share_c)
            heat = grad_t + c_ref[n, i, here] * grad_k
            absorbed = gain * (a[g] * l_ref[n, 9 * rf + g + 1, here] - (below + runs[g]))
            put(i, a[g] + (heat + r_ref[n, i, here] * (absorbed - heat)))
            push_before, share_before, before[g] = push, share, (push_r, share_r)


def backward(own, r1, r2, r3, t_ref, k_ref, c_ref, r_ref, l_ref, light, zid, a_ref, zpart, total):
    _gather((own, r1, r2, r3), a_ref.at[0], SEED_HALO, SEED_WIDE)
    fields = (t_ref, k_ref, c_ref, r_ref, l_ref, light)
    total[...] = jnp.zeros(total.shape, F32)

    def step(i, carry):
        n, at = 3 - i, lax.rem(i, 2)
        source, target = a_ref.at[at], a_ref.at[1 - at]
        _ghost(lambda j, c: source.at[j, pl.ds(BASE + c, 1)])
        tiles = _Tiles(BASE + SEED_HALO, SEED_WIDE, False)

        def put(j, value):
            target[j, tiles.here] = value

        def seen(rf, value):
            total[rf, tiles.here] += value

        _retreat(n, tiles, source, *fields, put, seen)
        return carry

    lax.fori_loop(0, 3, step, 0)
    source = a_ref.at[1]
    _ghost(lambda j, c: source.at[j, pl.ds(BASE + c, 1)])
    core = pl.ds(BASE + HALO, CORE)
    sums = []
    for rf in range(4):
        value = total[rf, core]
        for g in range(8):
            value = value + source[8 * rf + g, core] * (l_ref[0, 9 * rf + g, core] - l_ref[0, 9 * rf + g + 1, core])
        sums.append(value * DT)
    rows = []
    for z in range(NZONE):
        picked = [jnp.where(zid[rf] == float(z), sums[rf], 0.0) for rf in range(4)]
        rows.append(jnp.sum((picked[0] + picked[1]) + (picked[2] + picked[3]), axis=0, keepdims=True))
    spread = jnp.concatenate(rows + [jnp.zeros((128 - NZONE, 128), F32)], axis=0)
    zpart[...] = jnp.sum(spread.T, axis=0, keepdims=True)


def last_step(a_ref, t_ref, k_ref, c_ref, r_ref, l_ref, light, o0, o1, o2, o3):
    masks = [jnp.broadcast_to(m[0:1], (CORE, 128)) for m in _source_masks()]
    values = [None] * 32

    def put(i, value):
        values[i] = value

    tiles = _Tiles(BASE + HALO, CORE, True)
    _retreat(0, tiles, a_ref.at[1], t_ref, k_ref, c_ref, r_ref, l_ref, light, put, lambda rf, value: None)
    for g in range(8):
        turned = [values[g]] + [pltpu.roll(values[8 * rf + g], 32 * rf, 1) for rf in (1, 2, 3)]
        for k, out in enumerate((o0, o1, o2, o3)):
            out[g] = _pick(masks, k, turned)


def unpack(own, r1, r2, r3, parts, out, total, buf):
    d = lax.axis_index("dep")
    for k, block in enumerate((own, r1, r2, r3)):
        buf[:, _columns(lax.rem(d + 4 - k, 4))] = block[...]
    for g in range(8):
        plain = buf[g].T
        for p in range(4):
            rf = lax.rem(p + 4 - d, 4)
            for sub in range(4):
                out[8 * sub + g, pl.ds(rf, 8, stride=4)] = plain[32 * p + 8 * sub : 32 * p + 8 * sub + 8]
    total[...] = jnp.sum(parts[...], axis=(0, 1))[:NZONE]


def _around(x, k):
    return lax.ppermute(x, "dep", [(s, (s + k) % 4) for s in range(4)])


def _place(y, z, core, x):
    return ((y * 4 + z) * 2 + core) * 4 + x


def _meet(v, partner):
    pairs = []
    for y in range(4):
        for z in range(4):
            for core in range(2):
                for x in range(4):
                    pairs.append((_place(y, z, core, x), _place(*partner(y, z, core, x))))
    return v + lax.ppermute(v, ("lat", "dep"), pairs)


def _shape(*dims):
    return jax.ShapeDtypeStruct(dims, F32)


def _call(kernel, inputs, outs, scratch=(), aliases=None, cost=None):
    return pl.pallas_call(
        kernel,
        out_shape=tuple(outs),
        in_specs=[_full()] * len(inputs),
        out_specs=(_full(),) * len(outs),
        scratch_shapes=list(scratch),
        input_output_aliases=aliases or {},
        cost_estimate=cost,
        compiler_params=_params(),
        name=kernel.__name__,
    )(*inputs)


def _call_hbm(kernel, inputs, outs, scratch):
    return pl.pallas_call(
        kernel,
        out_shape=tuple(outs),
        in_specs=[pl.BlockSpec(memory_space=pltpu.HBM)] * len(inputs),
        out_specs=(_full(),) * len(outs),
        scratch_shapes=list(scratch),
        compiler_params=_params(),
        name=kernel.__name__,
    )(*[pltpu.with_memory_space_constraint(x, pltpu.HBM) for x in inputs])


def _swap(x, axes, places, first):
    return lax.ppermute(
        x, axes, [pair for a, b in list(zip(places, places[1:], strict=False))[first::2] for pair in ((a, b), (b, a))]
    )


def per_device(h, zones, fluence, seed):
    piece = _shape(8, CORE, 128)
    h0, h1, h2, h3 = _call_hbm(
        pack_state, (h,), (piece,) * 4, (_vmem(32, 32, 128), _vmem(8, 128, 128), pltpu.SemaphoreType.DMA)
    )
    h2, h1, h3 = _around(h2, 2), _around(h1, 1), _around(h3, 3)
    edge = _shape(8, 8, 128)
    start, light, zid, to_inner, to_outer = _call_hbm(
        pack_rest,
        (fluence, zones, seed),
        (_shape(8, 128, 128), _shape(4, 128, 128), _shape(4, CORE, 128), edge, edge),
        (
            _vmem(2, 8, 8, 128),
            _vmem(32, 32, 128),
            pltpu.VMEM((32, 128), jnp.int32),
            _vmem(2, 32, 128),
            _vmem(128, 128),
            pltpu.SMEM((NZONE,), F32),
            pltpu.SemaphoreType.DMA((3,)),
        ),
    )
    line = range(32)
    outer, inner = _swap(to_outer, "lat", line, 1), _swap(to_inner, "lat", line, 0)
    one = _vmem(32, HIGH, 128)
    side = _shape(32, HALO, 128)
    inner, outer, h0 = lax.optimization_barrier((inner, outer, h0))
    state, to_inner, to_outer = _call(gather_state, (h0, h1, h2, h3), (one, side, side))
    axes = ("lat", "dep")
    line = [4 * l + (c if l % 2 == 0 else 3 - c) for l in range(32) for c in range(4)]
    seed_block = _shape(8, SEED_WIDE, 128)
    start, to_inner = lax.optimization_barrier((start, to_inner))
    s0, s1, s2, s3, light = _call(
        insert,
        (start, light, inner, outer),
        (seed_block,) * 4 + (_shape(4, HIGH, 128),),
        (_vmem(2, 8, 8, 128), _vmem(8, 136, 128), _vmem(144, 128)),
    )
    outer, inner = _swap(to_outer, axes, line, 1), _swap(to_inner, axes, line, 0)
    s2, s1, s3 = _around(s2, 2), _around(s1, 1), _around(s3, 3)
    field = _vmem(4, 32, HIGH, 128)
    fields = (one,) * 2 + (field,) * 4 + (_vmem(4, 36, HIGH, 128),)
    states = _call(forward_core, (state, light), fields, cost=pl.CostEstimate(flops=1000, bytes_accessed=1000, transcendentals=0))
    states = _call(
        forward_sides,
        (inner, outer, light, state, *states),
        (one,) + fields,
        (),
        {3 + i: i for i in range(8)},
        pl.CostEstimate(flops=10000000000, bytes_accessed=100000000, transcendentals=0),
    )[3:]
    a, zpart = _call(
        backward,
        (s0, s1, s2, s3, *states, light, zid),
        (_vmem(2, 32, HIGH, 128), _shape(1, 128)),
        (_vmem(4, HIGH, 128),),
    )
    o0, o1, o2, o3 = _call(last_step, (a, *states, light), (piece,) * 4)
    o2, o1, o3 = _around(o2, 2), _around(o1, 1), _around(o3, 3)
    parts = lax.all_to_all(jnp.broadcast_to(zpart[None], (128, 1, 128)), axes, 0, 0)
    out, total = _call(unpack, (o0, o1, o2, o3, parts), (_shape(32, 32, 128), _shape(NZONE)), (_vmem(8, 128, 128),))
    return out, total


def solution(mesh):
    in_specs = (P("dep", None, "lat"), P(None, "lat"), P(), P("dep", None, "lat"))
    out_specs = (P("dep", None, "lat"), P())
    return jax.shard_map(per_device, mesh=mesh, in_specs=in_specs, out_specs=out_specs, check_vma=False)
```

```python
import math

import jax
import jax.numpy as jnp
from jax import lax
from jax.experimental import pallas as pl
from jax.experimental.pallas import tpu as pltpu
from jax.sharding import PartitionSpec as P


NZONE = 16
CORE = 32
HALO = 8
WIDE = CORE + 2 * HALO
SEED_HALO = 4
SEED_WIDE = CORE + 2 * SEED_HALO
BASE = 8
HIGH = WIDE + 2 * BASE
DT = 0.1
ABSORB_SOLID = 0.004
ABSORB_RISE = 0.026
LOG2E = math.log2(math.e)
EM10 = math.exp(-10.0)
F32 = jnp.float32


def _params():
    return pltpu.CompilerParams(vmem_limit_bytes=16 * 1024 * 1024)


def _group(d):
    return jnp.where(lax.rem(lax.axis_index("lat"), 2) == 0, d, 3 - d)


def _columns(d):
    return pl.ds(pl.multiple_of(_group(d) * CORE, CORE), CORE)


def _vmem(*shape):
    return pltpu.VMEM(shape, F32)


def _full():
    return pl.BlockSpec(memory_space=pltpu.VMEM)


def _lanes(rows=8):
    return lax.broadcasted_iota(jnp.int32, (rows, 128), 1)


def _packed(ref, g, d):
    tiles = []
    for p in range(4):
        rf = lax.rem(p + 4 - d, 4)
        tiles += [ref[8 * sub + g, pl.ds(rf, 8, stride=4)] for sub in range(4)]
    return jnp.concatenate(tiles, axis=0).T


def _surface(ref, rf):
    return jnp.concatenate([ref[pl.ds(rf, 8, stride=4)]] * 16, axis=0).T


def pack_state(h_in, h0, h1, h2, h3, h, buf, sem):
    d = lax.axis_index("dep")
    copy = pltpu.make_async_copy(h_in, h, sem)
    copy.start()
    copy.wait()
    for g in range(8):
        buf[g] = _packed(h, g, d)
    for k, out in enumerate((h0, h1, h2, h3)):
        out[...] = buf[:, _columns(lax.rem(d + k, 4))]


def pack_rest(fluence_in, zones_in, a_in, s0, s1, s2, s3, light, zid, a, zones, flat, buf, zbuf, fluence, sems):
    d = lax.axis_index("dep")
    copies = [
        pltpu.make_async_copy(source, target, sems.at[k])
        for k, (source, target) in enumerate(((fluence_in, fluence), (zones_in, zones), (a_in, a)))
    ]
    for copy in copies:
        copy.start()
    copies[0].wait()
    copies[1].wait()
    ids = zones[...]
    intensity = jnp.zeros(ids.shape, F32)
    for k in range(NZONE):
        intensity = jnp.where(ids == k, fluence[k] * DT, intensity)
    flat[0] = intensity
    flat[1] = ids.astype(F32)
    blank = jnp.zeros((BASE + HALO, 128), F32)
    for rf in range(4):
        zbuf[0] = _surface(flat.at[0], rf)
        light[rf, 0 : BASE + HALO] = blank
        light[rf, BASE + HALO : BASE + HALO + CORE] = zbuf[0, _columns(d)]
        light[rf, BASE + HALO + CORE :] = blank
        zbuf[1] = _surface(flat.at[1], rf)
        zid[rf] = zbuf[1, _columns(d)]
    copies[2].wait()
    for g in range(8):
        buf[g] = _packed(a, g, d)
    for k, out in enumerate((s0, s1, s2, s3)):
        out[...] = buf[:, _columns(lax.rem(d + k, 4))]


def _source_masks():
    part = lax.rem(_lanes(8) // 32 + 4 - lax.axis_index("dep"), 4)
    return [part == j for j in range(4)]


def _pick(masks, shift, values):
    return jnp.where(
        masks[shift % 4],
        values[0],
        jnp.where(masks[(shift + 1) % 4], values[1], jnp.where(masks[(shift + 2) % 4], values[2], values[3])),
    )


def _gather(blocks, field, first, count):
    masks = [jnp.broadcast_to(m[0:1], (count, 128)) for m in _source_masks()]
    for g in range(8):
        own, r1, r2, r3 = [block[g] for block in blocks]
        for rf in range(4):
            mixed = _pick(masks, rf, (own, r3, r2, r1))
            field[8 * rf + g, pl.ds(BASE + first, count)] = mixed if rf == 0 else pltpu.roll(mixed, 128 - 32 * rf, 1)


class _Tiles:
    def __init__(self, starts, count, exact):
        self.starts, self.count, self.exact = starts, count, exact
        self.rows = count * len(starts)

    def load(self, ref, *lead, shift=0):
        parts = [ref[(*lead, pl.ds(BASE + start + shift, self.count))] for start in self.starts]
        return parts[0] if len(parts) == 1 else jnp.concatenate(parts, axis=0)

    def store(self, value, ref, *lead):
        for k, start in enumerate(self.starts):
            ref[(*lead, pl.ds(BASE + start, self.count))] = value[k * self.count : (k + 1) * self.count]


def _inclusive(total, lane, reverse):
    a = lax.broadcasted_iota(jnp.int32, (128, 128), 0)
    b = lax.broadcasted_iota(jnp.int32, (128, 128), 1)
    same = lax.rem(a, 8) == lax.rem(b, 8)
    tri = jnp.where(jnp.logical_and(same, a >= b if reverse else a <= b), 1.0, 0.0).astype(jnp.bfloat16)
    high = total.astype(jnp.bfloat16)
    low = (total - high.astype(F32)).astype(jnp.bfloat16)
    return jnp.dot(high, tri, preferred_element_type=F32) + jnp.dot(low, tri, preferred_element_type=F32)


def _properties(n, rf, tiles, states, t_ref, k_ref, c_ref, r_ref, l_ref):
    lane = _lanes(tiles.rows)
    run = jnp.zeros((tiles.rows, 128), F32)
    runs = []
    for g in range(8):
        i = 8 * rf + g
        h = states[g]
        e = jnp.exp2(h * (10.0 * LOG2E) - 10.0 * LOG2E)
        u = 1.0 + e
        v = 1.0 + EM10 * e
        inv = pl.reciprocal(u * v)
        ramp = 0.1 * jnp.log(u * (u * inv))
        t = h - ramp
        m = pl.reciprocal(1.0 + t * t)
        tiles.store(t, t_ref, n, i)
        tiles.store(0.03 + 0.04 * m, k_ref, n, i)
        tiles.store((-0.08 * t) * (m * m), c_ref, n, i)
        tiles.store(e * ((1.0 - EM10) * inv), r_ref, n, i)
        runs.append(run)
        run = run + (ABSORB_SOLID * LOG2E + (ABSORB_RISE * LOG2E) * ramp)
    above = _inclusive(run, lane, False) - run
    for g in range(8):
        tiles.store(jnp.exp2(-(above + runs[g])), l_ref, n, 9 * rf + g)
    tiles.store(jnp.exp2(-(above + run)), l_ref, n, 9 * rf + 8)


def _advance(n, tiles, h_ref, t_ref, k_ref, l_ref, light, then):
    lane = _lanes(tiles.rows)
    inside = lax.rem(lane, 8) < 7
    above_bottom = lane < 120

    def across(g):
        t3, k3 = tiles.load(t_ref, n, 24 + g), tiles.load(k_ref, n, 24 + g)
        t0, k0 = pltpu.roll(tiles.load(t_ref, n, g), 127, 1), pltpu.roll(tiles.load(k_ref, n, g), 127, 1)
        return jnp.where(inside, (k3 + k0) * (t0 - t3), 0.0)

    last = [across(g) for g in range(8)]
    before = [pltpu.roll(f, 1, 1) for f in last]
    for rf in range(4):
        i0 = 8 * rf
        t = [tiles.load(t_ref, n, i0 + g) for g in range(8)]
        k = [tiles.load(k_ref, n, i0 + g) for g in range(8)]
        end = jnp.where(above_bottom, (k[7] + pltpu.roll(k[0], 120, 1)) * (pltpu.roll(t[0], 120, 1) - t[7]), 0.0)
        flux_before = pltpu.roll(end, 8, 1)
        new = []
        for g in range(8):
            i = i0 + g
            if g < 7:
                flux = (k[g] + k[g + 1]) * (t[g + 1] - t[g])
            else:
                flux = jnp.where(above_bottom, end, -0.05 * t[7])
            if rf < 3:
                side = (k[g] + tiles.load(k_ref, n, i + 8)) * (tiles.load(t_ref, n, i + 8) - t[g])
            else:
                side = last[g]
            change = (flux - flux_before) + (side - before[g])
            col = (k[g] + tiles.load(k_ref, n, i, shift=1)) * (tiles.load(t_ref, n, i, shift=1) - t[g])
            if tiles.exact:
                col_before = (tiles.load(k_ref, n, i, shift=-1) + k[g]) * (t[g] - tiles.load(t_ref, n, i, shift=-1))
            else:
                col_before = pltpu.roll(col, 1, 0)
            change = change + (col - col_before)
            source = tiles.load(light, rf) * (tiles.load(l_ref, n, 9 * rf + g) - tiles.load(l_ref, n, 9 * rf + g + 1))
            new.append(tiles.load(h_ref, i) + (change + source))
            flux_before, before[g] = flux, side
        then(rf, new)


def _ghost(ref_rows):
    lat, group = lax.axis_index("lat"), _group(lax.axis_index("dep"))

    @pl.when(jnp.logical_and(lat == 0, group == 0))
    def _():
        for i in range(32):
            ref_rows(i, HALO - 1)[...] = ref_rows(i, HALO)[...]

    @pl.when(jnp.logical_and(lat == 31, group == 3))
    def _():
        for i in range(32):
            ref_rows(i, HALO + CORE)[...] = ref_rows(i, HALO + CORE - 1)[...]


def gather_state(own, r1, r2, r3, h0):
    _gather((own, r1, r2, r3), h0, HALO, CORE)


def gather_seed(own, r1, r2, r3, h0, light, a_ref, to_inner, to_outer, edges):
    _gather((own, r1, r2, r3), a_ref.at[0], HALO, CORE)
    for side, first, seed_first in ((0, HALO, HALO), (1, CORE, HALO + CORE - SEED_HALO)):
        edges[side, 0:32] = h0[:, BASE + first : BASE + first + HALO]
        for i in range(32):
            edges[side, 32 + i // 2, pl.ds(4 * (i % 2), 4)] = a_ref[0, i, pl.ds(BASE + seed_first, SEED_HALO)]
        edges[side, 48:52] = light[:, BASE + first : BASE + first + HALO]
    odd = lax.rem(_group(lax.axis_index("dep")), 2)
    to_inner[...] = edges[1 - odd]
    to_outer[...] = edges[odd]


def forward_core(h0, light, h1, h2, t_ref, k_ref, c_ref, r_ref, l_ref):
    fields = (t_ref, k_ref, c_ref, r_ref, l_ref)
    tiles = _Tiles((HALO,), CORE, False)
    for rf in range(4):
        _properties(0, rf, tiles, [tiles.load(h0, 8 * rf + g) for g in range(8)], *fields)
    for n, source, target in ((0, h0, h1), (1, h1, h2), (2, h2, None)):

        def then(rf, new, n=n, target=target):
            if target is not None:
                for g in range(8):
                    tiles.store(new[g], target, 8 * rf + g)
            _properties(n + 1, rf, tiles, new, *fields)

        _advance(n, tiles, source, t_ref, k_ref, l_ref, light, then)


def _retreat(n, tiles, a_ref, t_ref, k_ref, c_ref, r_ref, l_ref, light, put):
    lane = _lanes(tiles.rows)
    inside = lax.rem(lane, 8) < 7
    above_bottom = lane < 120

    def across(g):
        a3, t3, k3 = tiles.load(a_ref, 24 + g), tiles.load(t_ref, n, 24 + g), tiles.load(k_ref, n, 24 + g)
        a0, t0, k0 = [pltpu.roll(x, 127, 1) for x in (tiles.load(a_ref, g), tiles.load(t_ref, n, g), tiles.load(k_ref, n, g))]
        jump = jnp.where(inside, a3 - a0, 0.0)
        return jump * (k3 + k0), jump * (t0 - t3)

    last = [across(g) for g in range(8)]
    before = [(pltpu.roll(push, 1, 1), pltpu.roll(share, 1, 1)) for push, share in last]
    for rf in range(4):
        i0 = 8 * rf
        a = [tiles.load(a_ref, i0 + g) for g in range(8)]
        t = [tiles.load(t_ref, n, i0 + g) for g in range(8)]
        k = [tiles.load(k_ref, n, i0 + g) for g in range(8)]
        run = jnp.zeros((tiles.rows, 128), F32)
        runs = [None] * 8
        for g in reversed(range(8)):
            runs[g] = run
            run = run + a[g] * (tiles.load(l_ref, n, 9 * rf + g) - tiles.load(l_ref, n, 9 * rf + g + 1))
        below = _inclusive(run, lane, True) - run
        gain = ABSORB_RISE * tiles.load(light, rf)
        jump = jnp.where(above_bottom, a[7] - pltpu.roll(a[0], 120, 1), 0.0)
        push_end = jump * (k[7] + pltpu.roll(k[0], 120, 1))
        share_end = jump * (pltpu.roll(t[0], 120, 1) - t[7])
        push_before, share_before = pltpu.roll(push_end, 8, 1), pltpu.roll(share_end, 8, 1)
        for g in range(8):
            i = i0 + g
            if g < 7:
                jump = a[g] - a[g + 1]
                push, share = jump * (k[g] + k[g + 1]), jump * (t[g + 1] - t[g])
            else:
                push, share = jnp.where(above_bottom, push_end, 0.05 * a[7]), share_end
            if rf < 3:
                jump = a[g] - tiles.load(a_ref, i + 8)
                push_r, share_r = jump * (k[g] + tiles.load(k_ref, n, i + 8)), jump * (tiles.load(t_ref, n, i + 8) - t[g])
            else:
                push_r, share_r = last[g]
            grad_t = (push_before - push) + (before[g][0] - push_r)
            grad_k = (share_before + share) + (before[g][1] + share_r)
            jump = a[g] - tiles.load(a_ref, i, shift=1)
            push_c, share_c = jump * (k[g] + tiles.load(k_ref, n, i, shift=1)), jump * (tiles.load(t_ref, n, i, shift=1) - t[g])
            if tiles.exact:
                jump = tiles.load(a_ref, i, shift=-1) - a[g]
                push_d, share_d = jump * (tiles.load(k_ref, n, i, shift=-1) + k[g]), jump * (t[g] - tiles.load(t_ref, n, i, shift=-1))
            else:
                push_d, share_d = pltpu.roll(push_c, 1, 0), pltpu.roll(share_c, 1, 0)
            grad_t = grad_t + (push_d - push_c)
            grad_k = grad_k + (share_d + share_c)
            heat = grad_t + tiles.load(c_ref, n, i) * grad_k
            absorbed = gain * (a[g] * tiles.load(l_ref, n, 9 * rf + g + 1) - (below + runs[g]))
            put(i, a[g] + (heat + tiles.load(r_ref, n, i) * (absorbed - heat)))
            push_before, share_before, before[g] = push, share, (push_r, share_r)


def backward_core(a_in, t_ref, k_ref, c_ref, r_ref, l_ref, light, a_ref):
    tiles = _Tiles((HALO,), CORE, False)

    def step(i, carry):
        def put(j, value):
            tiles.store(value, a_ref, i + 1, j)

        _retreat(3 - i, tiles, a_ref.at[i], t_ref, k_ref, c_ref, r_ref, l_ref, light, put)
        return carry

    lax.fori_loop(0, 3, step, 0)


def sides(inner, outer, zid, *refs):
    zpart, h0, h1, h2, t_ref, k_ref, c_ref, r_ref, l_ref, light, a_ref = refs[10:]
    fields = (t_ref, k_ref, c_ref, r_ref, l_ref)
    even = lax.rem(_group(lax.axis_index("dep")), 2) == 0

    def place(left, right):
        for edge, first, seed_first in ((left, 0, SEED_HALO), (right, HALO + CORE, HALO + CORE)):
            h0[:, BASE + first : BASE + first + HALO] = edge[0:32]
            for i in range(32):
                a_ref[0, i, pl.ds(BASE + seed_first, SEED_HALO)] = edge[32 + i // 2, pl.ds(4 * (i % 2), 4)]
            light[:, BASE + first : BASE + first + HALO] = edge[48:52]

    @pl.when(even)
    def _():
        place(outer, inner)

    @pl.when(jnp.logical_not(even))
    def _():
        place(inner, outer)

    tiles = _Tiles((0, HALO + CORE), HALO, True)
    for rf in range(4):
        _properties(0, rf, tiles, [tiles.load(h0, 8 * rf + g) for g in range(8)], *fields)
    for n, source, target in ((0, h0, h1), (1, h1, h2), (2, h2, None)):
        _ghost(lambda i, c, n=n: t_ref.at[n, i, pl.ds(BASE + c, 1)])
        tiles = _Tiles((n + 1, HALO + CORE - 1 - n), HALO, True)

        def then(rf, new, n=n, target=target, tiles=tiles):
            if target is not None:
                for g in range(8):
                    tiles.store(new[g], target, 8 * rf + g)
            _properties(n + 1, rf, tiles, new, *fields)

        _advance(n, tiles, source, t_ref, k_ref, l_ref, light, then)
    for m in range(3):
        _ghost(lambda i, c, m=m: a_ref.at[m, i, pl.ds(BASE + c, 1)])
        tiles = _Tiles((SEED_HALO + m, HALO + CORE - SEED_HALO - m), HALO, True)

        def put(j, value, m=m, tiles=tiles):
            tiles.store(value, a_ref, m + 1, j)

        _retreat(3 - m, tiles, a_ref.at[m], *fields, light, put)
    _ghost(lambda i, c: a_ref.at[3, i, pl.ds(BASE + c, 1)])
    core = pl.ds(BASE + HALO, CORE)
    rows = []
    sums = []
    for rf in range(4):
        value = jnp.zeros((CORE, 128), F32)
        for n in range(4):
            for g in range(8):
                lost = l_ref[n, 9 * rf + g, core] - l_ref[n, 9 * rf + g + 1, core]
                value = value + a_ref[3 - n, 8 * rf + g, core] * lost
        sums.append(value * DT)
    for z in range(NZONE):
        picked = [jnp.where(zid[rf] == float(z), sums[rf], 0.0) for rf in range(4)]
        rows.append(jnp.sum((picked[0] + picked[1]) + (picked[2] + picked[3]), axis=0, keepdims=True))
    spread = jnp.concatenate(rows + [jnp.zeros((128 - NZONE, 128), F32)], axis=0)
    zpart[...] = jnp.sum(spread.T, axis=0, keepdims=True)


def last_step(a_ref, t_ref, k_ref, c_ref, r_ref, l_ref, light, o0, o1, o2, o3):
    masks = [jnp.broadcast_to(m[0:1], (CORE, 128)) for m in _source_masks()]
    values = [None] * 32

    def put(i, value):
        values[i] = value

    tiles = _Tiles((HALO,), CORE, True)
    _retreat(0, tiles, a_ref.at[3], t_ref, k_ref, c_ref, r_ref, l_ref, light, put)
    for g in range(8):
        turned = [values[g]] + [pltpu.roll(values[8 * rf + g], 32 * rf, 1) for rf in (1, 2, 3)]
        for k, out in enumerate((o0, o1, o2, o3)):
            out[g] = _pick(masks, k, turned)


def unpack(own, r1, r2, r3, parts, out, total, buf):
    d = lax.axis_index("dep")
    for k, block in enumerate((own, r1, r2, r3)):
        buf[:, _columns(lax.rem(d + 4 - k, 4))] = block[...]
    for g in range(8):
        plain = buf[g].T
        for p in range(4):
            rf = lax.rem(p + 4 - d, 4)
            for sub in range(4):
                out[8 * sub + g, pl.ds(rf, 8, stride=4)] = plain[32 * p + 8 * sub : 32 * p + 8 * sub + 8]
    total[...] = jnp.sum(parts[...], axis=(0, 1))[:NZONE]


def _around(x, k):
    return lax.ppermute(x, "dep", [(s, (s + k) % 4) for s in range(4)])


def _place(y, z, core, x):
    return ((y * 4 + z) * 2 + core) * 4 + x


def _meet(v, partner):
    pairs = []
    for y in range(4):
        for z in range(4):
            for core in range(2):
                for x in range(4):
                    pairs.append((_place(y, z, core, x), _place(*partner(y, z, core, x))))
    return v + lax.ppermute(v, ("lat", "dep"), pairs)


def _shape(*dims):
    return jax.ShapeDtypeStruct(dims, F32)


def _call(kernel, inputs, outs, scratch=(), aliases=None, cost=None):
    return pl.pallas_call(
        kernel,
        out_shape=tuple(outs),
        in_specs=[_full()] * len(inputs),
        out_specs=(_full(),) * len(outs),
        scratch_shapes=list(scratch),
        input_output_aliases=aliases or {},
        cost_estimate=cost,
        compiler_params=_params(),
        name=kernel.__name__,
    )(*inputs)


def _call_hbm(kernel, inputs, outs, scratch):
    return pl.pallas_call(
        kernel,
        out_shape=tuple(outs),
        in_specs=[pl.BlockSpec(memory_space=pltpu.HBM)] * len(inputs),
        out_specs=(_full(),) * len(outs),
        scratch_shapes=list(scratch),
        compiler_params=_params(),
        name=kernel.__name__,
    )(*[pltpu.with_memory_space_constraint(x, pltpu.HBM) for x in inputs])


def _swap(x, axes, places, first):
    return lax.ppermute(
        x, axes, [pair for a, b in list(zip(places, places[1:], strict=False))[first::2] for pair in ((a, b), (b, a))]
    )


def per_device(h, zones, fluence, seed):
    piece = _shape(8, CORE, 128)
    h0, h1, h2, h3 = _call_hbm(
        pack_state, (h,), (piece,) * 4, (_vmem(32, 32, 128), _vmem(8, 128, 128), pltpu.SemaphoreType.DMA)
    )
    h2, h1, h3 = _around(h2, 2), _around(h1, 1), _around(h3, 3)
    surface = _vmem(4, HIGH, 128)
    s0, s1, s2, s3, light, zid = _call_hbm(
        pack_rest,
        (fluence, zones, seed),
        (piece,) * 4 + (surface, _shape(4, CORE, 128)),
        (
            _vmem(32, 32, 128),
            pltpu.VMEM((32, 128), jnp.int32),
            _vmem(2, 32, 128),
            _vmem(8, 128, 128),
            _vmem(2, 128, 128),
            pltpu.SMEM((NZONE,), F32),
            pltpu.SemaphoreType.DMA((3,)),
        ),
    )
    s2, s1, s3 = _around(s2, 2), _around(s1, 1), _around(s3, 3)
    one, four = _vmem(32, HIGH, 128), _vmem(4, 32, HIGH, 128)
    fields = (one, one, four, four, four, four, _vmem(4, 36, HIGH, 128))
    (state,) = _call(gather_state, (h0, h1, h2, h3), (one,))
    states = _call(forward_core, (state, light), fields)
    edge = _shape(52, HALO, 128)
    s0, light, *states = lax.optimization_barrier((s0, light, *states))
    a, to_inner, to_outer = _call(
        gather_seed, (s0, s1, s2, s3, state, light), (four, edge, edge), (_vmem(2, 52, HALO, 128),)
    )
    axes = ("lat", "dep")
    line = [4 * l + (c if l % 2 == 0 else 3 - c) for l in range(32) for c in range(4)]
    outer, inner = _swap(to_outer, axes, line, 1), _swap(to_inner, axes, line, 0)
    (a,) = _call(backward_core, (a, *states[2:], light), (four,), (), {0: 0})
    zpart, *states = _call(
        sides,
        (inner, outer, zid, state, *states, light, a),
        (_shape(1, 128), one) + fields + (surface, four),
        (),
        {3 + i: 1 + i for i in range(10)},
    )
    o0, o1, o2, o3 = _call(last_step, (states[9], *states[3:9]), (piece,) * 4)
    o2, o1, o3 = _around(o2, 2), _around(o1, 1), _around(o3, 3)
    parts = lax.all_to_all(jnp.broadcast_to(zpart[None], (128, 1, 128)), axes, 0, 0)
    out, total = _call(unpack, (o0, o1, o2, o3, parts), (_shape(32, 32, 128), _shape(NZONE)), (_vmem(8, 128, 128),))
    return out, total


def solution(mesh):
    in_specs = (P("dep", None, "lat"), P(None, "lat"), P(), P("dep", None, "lat"))
    out_specs = (P("dep", None, "lat"), P())
    return jax.shard_map(per_device, mesh=mesh, in_specs=in_specs, out_specs=out_specs, check_vma=False)
```

```python
import math

import jax
import jax.numpy as jnp
from jax import lax
from jax.experimental import pallas as pl
from jax.experimental.pallas import tpu as pltpu
from jax.sharding import PartitionSpec as P


NZONE = 16
CORE = 32
HALO = 8
WIDE = CORE + 2 * HALO
SEED_HALO = 4
SEED_WIDE = CORE + 2 * SEED_HALO
BASE = 8
HIGH = WIDE + 2 * BASE
DT = 0.1
ABSORB_SOLID = 0.004
ABSORB_RISE = 0.026
LOG2E = math.log2(math.e)
EM10 = math.exp(-10.0)
F32 = jnp.float32


def _params():
    return pltpu.CompilerParams(vmem_limit_bytes=16 * 1024 * 1024)


def _group(d):
    return jnp.where(lax.rem(lax.axis_index("lat"), 2) == 0, d, 3 - d)


def _columns(d):
    return pl.ds(pl.multiple_of(_group(d) * CORE, CORE), CORE)


def _vmem(*shape):
    return pltpu.VMEM(shape, F32)


def _full():
    return pl.BlockSpec(memory_space=pltpu.VMEM)


def _lanes(rows=8):
    return lax.broadcasted_iota(jnp.int32, (rows, 128), 1)


def _packed(ref, g, d):
    tiles = []
    for p in range(4):
        rf = lax.rem(p + 4 - d, 4)
        tiles += [ref[8 * sub + g, pl.ds(rf, 8, stride=4)] for sub in range(4)]
    return jnp.concatenate(tiles, axis=0).T


def _surface(ref, rf):
    return jnp.concatenate([ref[pl.ds(rf, 8, stride=4)]] * 16, axis=0).T


def pack_state(h_in, h0, h1, h2, h3, h, buf, sem):
    d = lax.axis_index("dep")
    copy = pltpu.make_async_copy(h_in, h, sem)
    copy.start()
    copy.wait()
    for g in range(8):
        buf[g] = _packed(h, g, d)
    for k, out in enumerate((h0, h1, h2, h3)):
        out[...] = buf[:, _columns(lax.rem(d + k, 4))]


def pack_rest(fluence_in, zones_in, a_in, s0, s1, s2, s3, light, zid, a, zones, flat, buf, zbuf, fluence, sems):
    d = lax.axis_index("dep")
    copies = [
        pltpu.make_async_copy(source, target, sems.at[k])
        for k, (source, target) in enumerate(((fluence_in, fluence), (zones_in, zones), (a_in, a)))
    ]
    for copy in copies:
        copy.start()
    copies[0].wait()
    copies[1].wait()
    ids = zones[...]
    intensity = jnp.zeros(ids.shape, F32)
    for k in range(NZONE):
        intensity = jnp.where(ids == k, fluence[k] * DT, intensity)
    flat[0] = intensity
    flat[1] = ids.astype(F32)
    blank = jnp.zeros((BASE + HALO, 128), F32)
    for rf in range(4):
        zbuf[0] = _surface(flat.at[0], rf)
        light[rf, 0 : BASE + HALO] = blank
        light[rf, BASE + HALO : BASE + HALO + CORE] = zbuf[0, _columns(d)]
        light[rf, BASE + HALO + CORE :] = blank
        zbuf[1] = _surface(flat.at[1], rf)
        zid[rf] = zbuf[1, _columns(d)]
    copies[2].wait()
    for g in range(8):
        buf[g] = _packed(a, g, d)
    for k, out in enumerate((s0, s1, s2, s3)):
        out[...] = buf[:, _columns(lax.rem(d + k, 4))]


def _source_masks():
    part = lax.rem(_lanes(8) // 32 + 4 - lax.axis_index("dep"), 4)
    return [part == j for j in range(4)]


def _pick(masks, shift, values):
    return jnp.where(
        masks[shift % 4],
        values[0],
        jnp.where(masks[(shift + 1) % 4], values[1], jnp.where(masks[(shift + 2) % 4], values[2], values[3])),
    )


def _gather(blocks, field, first, count):
    masks = [jnp.broadcast_to(m[0:1], (count, 128)) for m in _source_masks()]
    for g in range(8):
        own, r1, r2, r3 = [block[g] for block in blocks]
        for rf in range(4):
            mixed = _pick(masks, rf, (own, r3, r2, r1))
            field[8 * rf + g, pl.ds(BASE + first, count)] = mixed if rf == 0 else pltpu.roll(mixed, 128 - 32 * rf, 1)


class _Tiles:
    def __init__(self, starts, count, exact):
        self.starts, self.count, self.exact = starts, count, exact
        self.rows = count * len(starts)

    def load(self, ref, *lead, shift=0):
        parts = [ref[(*lead, pl.ds(BASE + start + shift, self.count))] for start in self.starts]
        return parts[0] if len(parts) == 1 else jnp.concatenate(parts, axis=0)

    def store(self, value, ref, *lead):
        for k, start in enumerate(self.starts):
            ref[(*lead, pl.ds(BASE + start, self.count))] = value[k * self.count : (k + 1) * self.count]


def _inclusive(total, lane, reverse):
    a = lax.broadcasted_iota(jnp.int32, (128, 128), 0)
    b = lax.broadcasted_iota(jnp.int32, (128, 128), 1)
    same = lax.rem(a, 8) == lax.rem(b, 8)
    tri = jnp.where(jnp.logical_and(same, a >= b if reverse else a <= b), 1.0, 0.0).astype(jnp.bfloat16)
    high = total.astype(jnp.bfloat16)
    low = (total - high.astype(F32)).astype(jnp.bfloat16)
    return jnp.dot(high, tri, preferred_element_type=F32) + jnp.dot(low, tri, preferred_element_type=F32)


def _properties(n, rf, tiles, states, t_ref, k_ref, c_ref, r_ref, l_ref):
    lane = _lanes(tiles.rows)
    run = jnp.zeros((tiles.rows, 128), F32)
    runs = []
    for g in range(8):
        i = 8 * rf + g
        h = states[g]
        e = jnp.exp2(h * (10.0 * LOG2E) - 10.0 * LOG2E)
        u = 1.0 + e
        v = 1.0 + EM10 * e
        inv = pl.reciprocal(u * v)
        ramp = 0.1 * jnp.log(u * (u * inv))
        t = h - ramp
        m = pl.reciprocal(1.0 + t * t)
        tiles.store(t, t_ref, n, i)
        tiles.store(0.03 + 0.04 * m, k_ref, n, i)
        tiles.store((-0.08 * t) * (m * m), c_ref, n, i)
        tiles.store(e * ((1.0 - EM10) * inv), r_ref, n, i)
        runs.append(run)
        run = run + (ABSORB_SOLID * LOG2E + (ABSORB_RISE * LOG2E) * ramp)
    above = _inclusive(run, lane, False) - run
    for g in range(8):
        tiles.store(jnp.exp2(-(above + runs[g])), l_ref, n, 9 * rf + g)
    tiles.store(jnp.exp2(-(above + run)), l_ref, n, 9 * rf + 8)


def _advance(n, tiles, h_ref, t_ref, k_ref, l_ref, light, then):
    lane = _lanes(tiles.rows)
    inside = lax.rem(lane, 8) < 7
    above_bottom = lane < 120

    def across(g):
        t3, k3 = tiles.load(t_ref, n, 24 + g), tiles.load(k_ref, n, 24 + g)
        t0, k0 = pltpu.roll(tiles.load(t_ref, n, g), 127, 1), pltpu.roll(tiles.load(k_ref, n, g), 127, 1)
        return jnp.where(inside, (k3 + k0) * (t0 - t3), 0.0)

    last = [across(g) for g in range(8)]
    before = [pltpu.roll(f, 1, 1) for f in last]
    for rf in range(4):
        i0 = 8 * rf
        t = [tiles.load(t_ref, n, i0 + g) for g in range(8)]
        k = [tiles.load(k_ref, n, i0 + g) for g in range(8)]
        end = jnp.where(above_bottom, (k[7] + pltpu.roll(k[0], 120, 1)) * (pltpu.roll(t[0], 120, 1) - t[7]), 0.0)
        flux_before = pltpu.roll(end, 8, 1)
        new = []
        for g in range(8):
            i = i0 + g
            if g < 7:
                flux = (k[g] + k[g + 1]) * (t[g + 1] - t[g])
            else:
                flux = jnp.where(above_bottom, end, -0.05 * t[7])
            if rf < 3:
                side = (k[g] + tiles.load(k_ref, n, i + 8)) * (tiles.load(t_ref, n, i + 8) - t[g])
            else:
                side = last[g]
            change = (flux - flux_before) + (side - before[g])
            col = (k[g] + tiles.load(k_ref, n, i, shift=1)) * (tiles.load(t_ref, n, i, shift=1) - t[g])
            if tiles.exact:
                col_before = (tiles.load(k_ref, n, i, shift=-1) + k[g]) * (t[g] - tiles.load(t_ref, n, i, shift=-1))
            else:
                col_before = pltpu.roll(col, 1, 0)
            change = change + (col - col_before)
            source = tiles.load(light, rf) * (tiles.load(l_ref, n, 9 * rf + g) - tiles.load(l_ref, n, 9 * rf + g + 1))
            new.append(tiles.load(h_ref, i) + (change + source))
            flux_before, before[g] = flux, side
        then(rf, new)


def _ghost(ref_rows):
    lat, group = lax.axis_index("lat"), _group(lax.axis_index("dep"))

    @pl.when(jnp.logical_and(lat == 0, group == 0))
    def _():
        for i in range(32):
            ref_rows(i, HALO - 1)[...] = ref_rows(i, HALO)[...]

    @pl.when(jnp.logical_and(lat == 31, group == 3))
    def _():
        for i in range(32):
            ref_rows(i, HALO + CORE)[...] = ref_rows(i, HALO + CORE - 1)[...]


def gather_state(own, r1, r3, r2, h0):
    _gather((own, r1, r2, r3), h0, HALO, CORE)


def gather_seed(own, r1, r3, r2, h0, light, a_ref, to_inner, to_outer, edges):
    _gather((own, r1, r2, r3), a_ref.at[0], HALO, CORE)
    for side, first, seed_first in ((0, HALO, HALO), (1, CORE, HALO + CORE - SEED_HALO)):
        edges[side, 0:32] = h0[:, BASE + first : BASE + first + HALO]
        for i in range(32):
            edges[side, 32 + i // 2, pl.ds(4 * (i % 2), 4)] = a_ref[0, i, pl.ds(BASE + seed_first, SEED_HALO)]
        edges[side, 48:52] = light[:, BASE + first : BASE + first + HALO]
    odd = lax.rem(_group(lax.axis_index("dep")), 2)
    to_inner[...] = edges[1 - odd]
    to_outer[...] = edges[odd]


def forward_core(h0, light, h1, h2, t_ref, k_ref, c_ref, r_ref, l_ref):
    fields = (t_ref, k_ref, c_ref, r_ref, l_ref)
    tiles = _Tiles((HALO,), CORE, False)
    for rf in range(4):
        _properties(0, rf, tiles, [tiles.load(h0, 8 * rf + g) for g in range(8)], *fields)
    for n, source, target in ((0, h0, h1), (1, h1, h2), (2, h2, None)):

        def then(rf, new, n=n, target=target):
            if target is not None:
                for g in range(8):
                    tiles.store(new[g], target, 8 * rf + g)
            _properties(n + 1, rf, tiles, new, *fields)

        _advance(n, tiles, source, t_ref, k_ref, l_ref, light, then)


def _retreat(n, tiles, a_ref, t_ref, k_ref, c_ref, r_ref, l_ref, light, put):
    lane = _lanes(tiles.rows)
    inside = lax.rem(lane, 8) < 7
    above_bottom = lane < 120

    def across(g):
        a3, t3, k3 = tiles.load(a_ref, 24 + g), tiles.load(t_ref, n, 24 + g), tiles.load(k_ref, n, 24 + g)
        a0, t0, k0 = [pltpu.roll(x, 127, 1) for x in (tiles.load(a_ref, g), tiles.load(t_ref, n, g), tiles.load(k_ref, n, g))]
        jump = jnp.where(inside, a3 - a0, 0.0)
        return jump * (k3 + k0), jump * (t0 - t3)

    last = [across(g) for g in range(8)]
    before = [(pltpu.roll(push, 1, 1), pltpu.roll(share, 1, 1)) for push, share in last]
    for rf in range(4):
        i0 = 8 * rf
        a = [tiles.load(a_ref, i0 + g) for g in range(8)]
        t = [tiles.load(t_ref, n, i0 + g) for g in range(8)]
        k = [tiles.load(k_ref, n, i0 + g) for g in range(8)]
        run = jnp.zeros((tiles.rows, 128), F32)
        runs = [None] * 8
        for g in reversed(range(8)):
            runs[g] = run
            run = run + a[g] * (tiles.load(l_ref, n, 9 * rf + g) - tiles.load(l_ref, n, 9 * rf + g + 1))
        below = _inclusive(run, lane, True) - run
        gain = ABSORB_RISE * tiles.load(light, rf)
        jump = jnp.where(above_bottom, a[7] - pltpu.roll(a[0], 120, 1), 0.0)
        push_end = jump * (k[7] + pltpu.roll(k[0], 120, 1))
        share_end = jump * (pltpu.roll(t[0], 120, 1) - t[7])
        push_before, share_before = pltpu.roll(push_end, 8, 1), pltpu.roll(share_end, 8, 1)
        for g in range(8):
            i = i0 + g
            if g < 7:
                jump = a[g] - a[g + 1]
                push, share = jump * (k[g] + k[g + 1]), jump * (t[g + 1] - t[g])
            else:
                push, share = jnp.where(above_bottom, push_end, 0.05 * a[7]), share_end
            if rf < 3:
                jump = a[g] - tiles.load(a_ref, i + 8)
                push_r, share_r = jump * (k[g] + tiles.load(k_ref, n, i + 8)), jump * (tiles.load(t_ref, n, i + 8) - t[g])
            else:
                push_r, share_r = last[g]
            grad_t = (push_before - push) + (before[g][0] - push_r)
            grad_k = (share_before + share) + (before[g][1] + share_r)
            jump = a[g] - tiles.load(a_ref, i, shift=1)
            push_c, share_c = jump * (k[g] + tiles.load(k_ref, n, i, shift=1)), jump * (tiles.load(t_ref, n, i, shift=1) - t[g])
            if tiles.exact:
                jump = tiles.load(a_ref, i, shift=-1) - a[g]
                push_d, share_d = jump * (tiles.load(k_ref, n, i, shift=-1) + k[g]), jump * (t[g] - tiles.load(t_ref, n, i, shift=-1))
            else:
                push_d, share_d = pltpu.roll(push_c, 1, 0), pltpu.roll(share_c, 1, 0)
            grad_t = grad_t + (push_d - push_c)
            grad_k = grad_k + (share_d + share_c)
            heat = grad_t + tiles.load(c_ref, n, i) * grad_k
            absorbed = gain * (a[g] * tiles.load(l_ref, n, 9 * rf + g + 1) - (below + runs[g]))
            put(i, a[g] + (heat + tiles.load(r_ref, n, i) * (absorbed - heat)))
            push_before, share_before, before[g] = push, share, (push_r, share_r)


def backward_core(a_in, t_ref, k_ref, c_ref, r_ref, l_ref, light, a_ref):
    tiles = _Tiles((HALO,), CORE, False)

    def step(i, carry):
        def put(j, value):
            tiles.store(value, a_ref, i + 1, j)

        _retreat(3 - i, tiles, a_ref.at[i], t_ref, k_ref, c_ref, r_ref, l_ref, light, put)
        return carry

    lax.fori_loop(0, 4, step, 0)


def sides(inner, outer, zid, *refs):
    zpart, *outs = refs[10:15]
    h0, h1, h2, t_ref, k_ref, c_ref, r_ref, l_ref, light, a_ref = refs[15:]
    fields = (t_ref, k_ref, c_ref, r_ref, l_ref)
    even = lax.rem(_group(lax.axis_index("dep")), 2) == 0

    def place(left, right):
        for edge, first, seed_first in ((left, 0, SEED_HALO), (right, HALO + CORE, HALO + CORE)):
            h0[:, BASE + first : BASE + first + HALO] = edge[0:32]
            for i in range(32):
                a_ref[0, i, pl.ds(BASE + seed_first, SEED_HALO)] = edge[32 + i // 2, pl.ds(4 * (i % 2), 4)]
            light[:, BASE + first : BASE + first + HALO] = edge[48:52]

    @pl.when(even)
    def _():
        place(outer, inner)

    @pl.when(jnp.logical_not(even))
    def _():
        place(inner, outer)

    tiles = _Tiles((0, HALO + CORE), HALO, True)
    for rf in range(4):
        _properties(0, rf, tiles, [tiles.load(h0, 8 * rf + g) for g in range(8)], *fields)
    for n, source, target in ((0, h0, h1), (1, h1, h2), (2, h2, None)):
        _ghost(lambda i, c, n=n: t_ref.at[n, i, pl.ds(BASE + c, 1)])
        tiles = _Tiles((n + 1, HALO + CORE - 1 - n), HALO, True)

        def then(rf, new, n=n, target=target, tiles=tiles):
            if target is not None:
                for g in range(8):
                    tiles.store(new[g], target, 8 * rf + g)
            _properties(n + 1, rf, tiles, new, *fields)

        _advance(n, tiles, source, t_ref, k_ref, l_ref, light, then)
    for m in range(4):
        _ghost(lambda i, c, m=m: a_ref.at[m, i, pl.ds(BASE + c, 1)])
        tiles = _Tiles((SEED_HALO + m, HALO + CORE - SEED_HALO - m), HALO, True)

        def put(j, value, m=m, tiles=tiles):
            tiles.store(value, a_ref, m + 1, j)

        _retreat(3 - m, tiles, a_ref.at[m], *fields, light, put)
    core = pl.ds(BASE + HALO, CORE)
    rows = []
    sums = []
    for rf in range(4):
        value = jnp.zeros((CORE, 128), F32)
        for n in range(4):
            for g in range(8):
                lost = l_ref[n, 9 * rf + g, core] - l_ref[n, 9 * rf + g + 1, core]
                value = value + a_ref[3 - n, 8 * rf + g, core] * lost
        sums.append(value * DT)
    for z in range(NZONE):
        picked = [jnp.where(zid[rf] == float(z), sums[rf], 0.0) for rf in range(4)]
        rows.append(jnp.sum((picked[0] + picked[1]) + (picked[2] + picked[3]), axis=0, keepdims=True))
    spread = jnp.concatenate(rows + [jnp.zeros((128 - NZONE, 128), F32)], axis=0)
    zpart[...] = jnp.sum(spread.T, axis=0, keepdims=True)
    masks = [jnp.broadcast_to(m[0:1], (CORE, 128)) for m in _source_masks()]
    for g in range(8):
        turned = [a_ref[4, g, core]] + [pltpu.roll(a_ref[4, 8 * rf + g, core], 32 * rf, 1) for rf in (1, 2, 3)]
        for k, out in enumerate(outs):
            out[g] = _pick(masks, k, turned)


def unpack(own, r1, r2, r3, parts, out, total, buf):
    d = lax.axis_index("dep")
    for k, block in enumerate((own, r1, r2, r3)):
        buf[:, _columns(lax.rem(d + 4 - k, 4))] = block[...]
    for g in range(8):
        plain = buf[g].T
        for p in range(4):
            rf = lax.rem(p + 4 - d, 4)
            for sub in range(4):
                out[8 * sub + g, pl.ds(rf, 8, stride=4)] = plain[32 * p + 8 * sub : 32 * p + 8 * sub + 8]
    total[...] = jnp.sum(parts[...], axis=(0, 1))[:NZONE]


def _around(x, k):
    return lax.ppermute(x, "dep", [(s, (s + k) % 4) for s in range(4)])


def _place(y, z, core, x):
    return ((y * 4 + z) * 2 + core) * 4 + x


def _meet(v, partner):
    pairs = []
    for y in range(4):
        for z in range(4):
            for core in range(2):
                for x in range(4):
                    pairs.append((_place(y, z, core, x), _place(*partner(y, z, core, x))))
    return v + lax.ppermute(v, ("lat", "dep"), pairs)


def _shape(*dims):
    return jax.ShapeDtypeStruct(dims, F32)


def _call(kernel, inputs, outs, scratch=(), aliases=None, cost=None):
    return pl.pallas_call(
        kernel,
        out_shape=tuple(outs),
        in_specs=[_full()] * len(inputs),
        out_specs=(_full(),) * len(outs),
        scratch_shapes=list(scratch),
        input_output_aliases=aliases or {},
        cost_estimate=cost,
        compiler_params=_params(),
        name=kernel.__name__,
    )(*inputs)


def _call_hbm(kernel, inputs, outs, scratch):
    return pl.pallas_call(
        kernel,
        out_shape=tuple(outs),
        in_specs=[pl.BlockSpec(memory_space=pltpu.HBM)] * len(inputs),
        out_specs=(_full(),) * len(outs),
        scratch_shapes=list(scratch),
        compiler_params=_params(),
        name=kernel.__name__,
    )(*[pltpu.with_memory_space_constraint(x, pltpu.HBM) for x in inputs])


def _swap(x, axes, places, first):
    return lax.ppermute(
        x, axes, [pair for a, b in list(zip(places, places[1:], strict=False))[first::2] for pair in ((a, b), (b, a))]
    )


def per_device(h, zones, fluence, seed):
    piece = _shape(8, CORE, 128)
    h0, h1, h2, h3 = _call_hbm(
        pack_state, (h,), (piece,) * 4, (_vmem(32, 32, 128), _vmem(8, 128, 128), pltpu.SemaphoreType.DMA)
    )
    h2, h1, h3 = _around(h2, 2), _around(h1, 1), _around(h3, 3)
    surface = _vmem(4, HIGH, 128)
    s0, s1, s2, s3, light, zid = _call_hbm(
        pack_rest,
        (fluence, zones, seed),
        (piece,) * 4 + (surface, _shape(4, CORE, 128)),
        (
            _vmem(32, 32, 128),
            pltpu.VMEM((32, 128), jnp.int32),
            _vmem(2, 32, 128),
            _vmem(8, 128, 128),
            _vmem(2, 128, 128),
            pltpu.SMEM((NZONE,), F32),
            pltpu.SemaphoreType.DMA((3,)),
        ),
    )
    s2, s1, s3 = _around(s2, 2), _around(s1, 1), _around(s3, 3)
    one, four, five = _vmem(32, HIGH, 128), _vmem(4, 32, HIGH, 128), _vmem(5, 32, HIGH, 128)
    fields = (one, one, four, four, four, four, _vmem(4, 36, HIGH, 128))
    (state,) = _call(gather_state, (h0, h1, h3, h2), (one,))
    states = _call(forward_core, (state, light), fields)
    edge = _shape(52, HALO, 128)
    s0, light, *states = lax.optimization_barrier((s0, light, *states))
    a, to_inner, to_outer = _call(
        gather_seed, (s0, s1, s3, s2, state, light), (five, edge, edge), (_vmem(2, 52, HALO, 128),)
    )
    axes = ("lat", "dep")
    line = [4 * l + (c if l % 2 == 0 else 3 - c) for l in range(32) for c in range(4)]
    outer, inner = _swap(to_outer, axes, line, 1), _swap(to_inner, axes, line, 0)
    (a,) = _call(backward_core, (a, *states[2:], light), (five,), (), {0: 0})
    zpart, o0, o1, o2, o3 = _call(
        sides,
        (inner, outer, zid, state, *states, light, a),
        (_shape(1, 128),) + (piece,) * 4 + (one,) + fields + (surface, five),
        (),
        {3 + i: 5 + i for i in range(10)},
    )[:5]
    o2, o1, o3 = _around(o2, 2), _around(o1, 1), _around(o3, 3)
    parts = lax.all_to_all(jnp.broadcast_to(zpart[None], (128, 1, 128)), axes, 0, 0)
    out, total = _call(unpack, (o0, o1, o2, o3, parts), (_shape(32, 32, 128), _shape(NZONE)), (_vmem(8, 128, 128),))
    return out, total


def solution(mesh):
    in_specs = (P("dep", None, "lat"), P(None, "lat"), P(), P("dep", None, "lat"))
    out_specs = (P("dep", None, "lat"), P())
    return jax.shard_map(per_device, mesh=mesh, in_specs=in_specs, out_specs=out_specs, check_vma=False)
```

```python
import math

import jax
import jax.numpy as jnp
from jax import lax
from jax.experimental import pallas as pl
from jax.experimental.pallas import tpu as pltpu
from jax.sharding import PartitionSpec as P


NZONE = 16
CORE = 32
HALO = 8
WIDE = CORE + 2 * HALO
SEED_HALO = 4
SEED_WIDE = CORE + 2 * SEED_HALO
BASE = 8
HIGH = WIDE + 2 * BASE
DT = 0.1
ABSORB_SOLID = 0.004
ABSORB_RISE = 0.026
LOG2E = math.log2(math.e)
EM10 = math.exp(-10.0)
F32 = jnp.float32


def _params():
    return pltpu.CompilerParams(vmem_limit_bytes=16 * 1024 * 1024)


def _group(d):
    return jnp.where(lax.rem(lax.axis_index("lat"), 2) == 0, d, 3 - d)


def _columns(d):
    return pl.ds(pl.multiple_of(_group(d) * CORE, CORE), CORE)


def _vmem(*shape):
    return pltpu.VMEM(shape, F32)


def _full():
    return pl.BlockSpec(memory_space=pltpu.VMEM)


def _lanes(rows=8):
    return lax.broadcasted_iota(jnp.int32, (rows, 128), 1)


def _packed(ref, g, d):
    tiles = []
    for p in range(4):
        rf = lax.rem(p + 4 - d, 4)
        tiles += [ref[8 * sub + g, pl.ds(rf, 8, stride=4)] for sub in range(4)]
    return jnp.concatenate(tiles, axis=0).T


def _surface(ref, rf):
    return jnp.concatenate([ref[pl.ds(rf, 8, stride=4)]] * 16, axis=0).T


def pack_state(h_in, h0, h1, h2, h3, h, buf, sem):
    d = lax.axis_index("dep")
    copy = pltpu.make_async_copy(h_in, h, sem)
    copy.start()
    copy.wait()
    for g in range(8):
        buf[g] = _packed(h, g, d)
    for k, out in enumerate((h0, h1, h2, h3)):
        out[...] = buf[:, _columns(lax.rem(d + k, 4))]


def pack_rest(fluence_in, zones_in, a_in, s0, s1, s2, s3, light, zid, a, zones, flat, buf, zbuf, fluence, sems):
    d = lax.axis_index("dep")
    copies = [
        pltpu.make_async_copy(source, target, sems.at[k])
        for k, (source, target) in enumerate(((fluence_in, fluence), (zones_in, zones), (a_in, a)))
    ]
    for copy in copies:
        copy.start()
    copies[0].wait()
    copies[1].wait()
    ids = zones[...]
    intensity = jnp.zeros(ids.shape, F32)
    for k in range(NZONE):
        intensity = jnp.where(ids == k, fluence[k] * DT, intensity)
    flat[0] = intensity
    flat[1] = ids.astype(F32)
    blank = jnp.zeros((BASE + HALO, 128), F32)
    for rf in range(4):
        zbuf[0] = _surface(flat.at[0], rf)
        light[rf, 0 : BASE + HALO] = blank
        light[rf, BASE + HALO : BASE + HALO + CORE] = zbuf[0, _columns(d)]
        light[rf, BASE + HALO + CORE :] = blank
        zbuf[1] = _surface(flat.at[1], rf)
        zid[rf] = zbuf[1, _columns(d)]
    copies[2].wait()
    for g in range(8):
        buf[g] = _packed(a, g, d)
    for k, out in enumerate((s0, s1, s2, s3)):
        out[...] = buf[:, _columns(lax.rem(d + k, 4))]


def _source_masks():
    part = lax.rem(_lanes(8) // 32 + 4 - lax.axis_index("dep"), 4)
    return [part == j for j in range(4)]


def _pick(masks, shift, values):
    return jnp.where(
        masks[shift % 4],
        values[0],
        jnp.where(masks[(shift + 1) % 4], values[1], jnp.where(masks[(shift + 2) % 4], values[2], values[3])),
    )


def _gather(blocks, field, first, count):
    masks = [jnp.broadcast_to(m[0:1], (count, 128)) for m in _source_masks()]
    for g in range(8):
        own, r1, r2, r3 = [block[g] for block in blocks]
        for rf in range(4):
            mixed = _pick(masks, rf, (own, r3, r2, r1))
            field[8 * rf + g, pl.ds(BASE + first, count)] = mixed if rf == 0 else pltpu.roll(mixed, 128 - 32 * rf, 1)


class _Tiles:
    def __init__(self, starts, count, exact):
        self.starts, self.count, self.exact = starts, count, exact
        self.rows = count * len(starts)

    def load(self, ref, *lead, shift=0):
        parts = [ref[(*lead, pl.ds(BASE + start + shift, self.count))] for start in self.starts]
        return parts[0] if len(parts) == 1 else jnp.concatenate(parts, axis=0)

    def store(self, value, ref, *lead):
        for k, start in enumerate(self.starts):
            ref[(*lead, pl.ds(BASE + start, self.count))] = value[k * self.count : (k + 1) * self.count]


def _inclusive(total, lane, reverse):
    a = lax.broadcasted_iota(jnp.int32, (128, 128), 0)
    b = lax.broadcasted_iota(jnp.int32, (128, 128), 1)
    same = lax.rem(a, 8) == lax.rem(b, 8)
    tri = jnp.where(jnp.logical_and(same, a >= b if reverse else a <= b), 1.0, 0.0).astype(jnp.bfloat16)
    high = total.astype(jnp.bfloat16)
    low = (total - high.astype(F32)).astype(jnp.bfloat16)
    return jnp.dot(high, tri, preferred_element_type=F32) + jnp.dot(low, tri, preferred_element_type=F32)


def _properties(n, rf, tiles, states, t_ref, k_ref, c_ref, r_ref, l_ref):
    lane = _lanes(tiles.rows)
    run = jnp.zeros((tiles.rows, 128), F32)
    runs = []
    for g in range(8):
        i = 8 * rf + g
        h = states[g]
        e = jnp.exp2(h * (10.0 * LOG2E) - 10.0 * LOG2E)
        u = 1.0 + e
        v = 1.0 + EM10 * e
        inv = pl.reciprocal(u * v)
        ramp = 0.1 * jnp.log(u * (u * inv))
        t = h - ramp
        m = pl.reciprocal(1.0 + t * t)
        tiles.store(t, t_ref, n, i)
        tiles.store(0.03 + 0.04 * m, k_ref, n, i)
        tiles.store((-0.08 * t) * (m * m), c_ref, n, i)
        tiles.store(e * ((1.0 - EM10) * inv), r_ref, n, i)
        runs.append(run)
        run = run + (ABSORB_SOLID * LOG2E + (ABSORB_RISE * LOG2E) * ramp)
    above = _inclusive(run, lane, False) - run
    for g in range(8):
        tiles.store(jnp.exp2(-(above + runs[g])), l_ref, n, 9 * rf + g)
    tiles.store(jnp.exp2(-(above + run)), l_ref, n, 9 * rf + 8)


def _advance(n, tiles, h_ref, t_ref, k_ref, l_ref, light, then):
    lane = _lanes(tiles.rows)
    inside = lax.rem(lane, 8) < 7
    above_bottom = lane < 120

    def across(g):
        t3, k3 = tiles.load(t_ref, n, 24 + g), tiles.load(k_ref, n, 24 + g)
        t0, k0 = pltpu.roll(tiles.load(t_ref, n, g), 127, 1), pltpu.roll(tiles.load(k_ref, n, g), 127, 1)
        return jnp.where(inside, (k3 + k0) * (t0 - t3), 0.0)

    last = [across(g) for g in range(8)]
    before = [pltpu.roll(f, 1, 1) for f in last]
    for rf in range(4):
        i0 = 8 * rf
        t = [tiles.load(t_ref, n, i0 + g) for g in range(8)]
        k = [tiles.load(k_ref, n, i0 + g) for g in range(8)]
        end = jnp.where(above_bottom, (k[7] + pltpu.roll(k[0], 120, 1)) * (pltpu.roll(t[0], 120, 1) - t[7]), 0.0)
        flux_before = pltpu.roll(end, 8, 1)
        new = []
        for g in range(8):
            i = i0 + g
            if g < 7:
                flux = (k[g] + k[g + 1]) * (t[g + 1] - t[g])
            else:
                flux = jnp.where(above_bottom, end, -0.05 * t[7])
            if rf < 3:
                side = (k[g] + tiles.load(k_ref, n, i + 8)) * (tiles.load(t_ref, n, i + 8) - t[g])
            else:
                side = last[g]
            change = (flux - flux_before) + (side - before[g])
            col = (k[g] + tiles.load(k_ref, n, i, shift=1)) * (tiles.load(t_ref, n, i, shift=1) - t[g])
            if tiles.exact:
                col_before = (tiles.load(k_ref, n, i, shift=-1) + k[g]) * (t[g] - tiles.load(t_ref, n, i, shift=-1))
            else:
                col_before = pltpu.roll(col, 1, 0)
            change = change + (col - col_before)
            source = tiles.load(light, rf) * (tiles.load(l_ref, n, 9 * rf + g) - tiles.load(l_ref, n, 9 * rf + g + 1))
            new.append(tiles.load(h_ref, i) + (change + source))
            flux_before, before[g] = flux, side
        then(rf, new)


def _ghost(ref_rows):
    lat, group = lax.axis_index("lat"), _group(lax.axis_index("dep"))

    @pl.when(jnp.logical_and(lat == 0, group == 0))
    def _():
        for i in range(32):
            ref_rows(i, HALO - 1)[...] = ref_rows(i, HALO)[...]

    @pl.when(jnp.logical_and(lat == 31, group == 3))
    def _():
        for i in range(32):
            ref_rows(i, HALO + CORE)[...] = ref_rows(i, HALO + CORE - 1)[...]


def gather_state(own, r1, r3, r2, h0):
    _gather((own, r1, r2, r3), h0, HALO, CORE)


def gather_seed(own, r1, r3, r2, h0, light, a_ref, to_inner, to_outer, edges):
    _gather((own, r1, r2, r3), a_ref.at[0], HALO, CORE)
    for side, first, seed_first in ((0, HALO, HALO), (1, CORE, HALO + CORE - SEED_HALO)):
        edges[side, 0:32] = h0[:, BASE + first : BASE + first + HALO]
        for i in range(32):
            edges[side, 32 + i // 2, pl.ds(4 * (i % 2), 4)] = a_ref[0, i, pl.ds(BASE + seed_first, SEED_HALO)]
        edges[side, 48:52] = light[:, BASE + first : BASE + first + HALO]
    odd = lax.rem(_group(lax.axis_index("dep")), 2)
    to_inner[...] = edges[1 - odd]
    to_outer[...] = edges[odd]


def forward_core(h0, light, h1, h2, t_ref, k_ref, c_ref, r_ref, l_ref):
    fields = (t_ref, k_ref, c_ref, r_ref, l_ref)
    tiles = _Tiles((HALO,), CORE, False)
    for rf in range(4):
        _properties(0, rf, tiles, [tiles.load(h0, 8 * rf + g) for g in range(8)], *fields)
    for n, source, target in ((0, h0, h1), (1, h1, h2), (2, h2, None)):

        def then(rf, new, n=n, target=target):
            if target is not None:
                for g in range(8):
                    tiles.store(new[g], target, 8 * rf + g)
            _properties(n + 1, rf, tiles, new, *fields)

        _advance(n, tiles, source, t_ref, k_ref, l_ref, light, then)


def _retreat(n, tiles, a_ref, t_ref, k_ref, c_ref, r_ref, l_ref, light, put):
    lane = _lanes(tiles.rows)
    inside = lax.rem(lane, 8) < 7
    above_bottom = lane < 120

    def across(g):
        a3, t3, k3 = tiles.load(a_ref, 24 + g), tiles.load(t_ref, n, 24 + g), tiles.load(k_ref, n, 24 + g)
        a0, t0, k0 = [pltpu.roll(x, 127, 1) for x in (tiles.load(a_ref, g), tiles.load(t_ref, n, g), tiles.load(k_ref, n, g))]
        jump = jnp.where(inside, a3 - a0, 0.0)
        return jump * (k3 + k0), jump * (t0 - t3)

    last = [across(g) for g in range(8)]
    before = [(pltpu.roll(push, 1, 1), pltpu.roll(share, 1, 1)) for push, share in last]
    for rf in range(4):
        i0 = 8 * rf
        a = [tiles.load(a_ref, i0 + g) for g in range(8)]
        t = [tiles.load(t_ref, n, i0 + g) for g in range(8)]
        k = [tiles.load(k_ref, n, i0 + g) for g in range(8)]
        run = jnp.zeros((tiles.rows, 128), F32)
        runs = [None] * 8
        for g in reversed(range(8)):
            runs[g] = run
            run = run + a[g] * (tiles.load(l_ref, n, 9 * rf + g) - tiles.load(l_ref, n, 9 * rf + g + 1))
        below = _inclusive(run, lane, True) - run
        gain = ABSORB_RISE * tiles.load(light, rf)
        jump = jnp.where(above_bottom, a[7] - pltpu.roll(a[0], 120, 1), 0.0)
        push_end = jump * (k[7] + pltpu.roll(k[0], 120, 1))
        share_end = jump * (pltpu.roll(t[0], 120, 1) - t[7])
        push_before, share_before = pltpu.roll(push_end, 8, 1), pltpu.roll(share_end, 8, 1)
        for g in range(8):
            i = i0 + g
            if g < 7:
                jump = a[g] - a[g + 1]
                push, share = jump * (k[g] + k[g + 1]), jump * (t[g + 1] - t[g])
            else:
                push, share = jnp.where(above_bottom, push_end, 0.05 * a[7]), share_end
            if rf < 3:
                jump = a[g] - tiles.load(a_ref, i + 8)
                push_r, share_r = jump * (k[g] + tiles.load(k_ref, n, i + 8)), jump * (tiles.load(t_ref, n, i + 8) - t[g])
            else:
                push_r, share_r = last[g]
            grad_t = (push_before - push) + (before[g][0] - push_r)
            grad_k = (share_before + share) + (before[g][1] + share_r)
            jump = a[g] - tiles.load(a_ref, i, shift=1)
            push_c, share_c = jump * (k[g] + tiles.load(k_ref, n, i, shift=1)), jump * (tiles.load(t_ref, n, i, shift=1) - t[g])
            if tiles.exact:
                jump = tiles.load(a_ref, i, shift=-1) - a[g]
                push_d, share_d = jump * (tiles.load(k_ref, n, i, shift=-1) + k[g]), jump * (t[g] - tiles.load(t_ref, n, i, shift=-1))
            else:
                push_d, share_d = pltpu.roll(push_c, 1, 0), pltpu.roll(share_c, 1, 0)
            grad_t = grad_t + (push_d - push_c)
            grad_k = grad_k + (share_d + share_c)
            heat = grad_t + tiles.load(c_ref, n, i) * grad_k
            absorbed = gain * (a[g] * tiles.load(l_ref, n, 9 * rf + g + 1) - (below + runs[g]))
            put(i, a[g] + (heat + tiles.load(r_ref, n, i) * (absorbed - heat)))
            push_before, share_before, before[g] = push, share, (push_r, share_r)


def backward_core(a_in, t_ref, k_ref, c_ref, r_ref, l_ref, light, a_ref):
    tiles = _Tiles((HALO,), CORE, False)

    def step(i, carry):
        def put(j, value):
            tiles.store(value, a_ref, i + 1, j)

        _retreat(3 - i, tiles, a_ref.at[i], t_ref, k_ref, c_ref, r_ref, l_ref, light, put)
        return carry

    lax.fori_loop(0, 4, step, 0)


def sides(inner, outer, zid, *refs):
    zpart, *outs = refs[10:15]
    h0, h1, h2, t_ref, k_ref, c_ref, r_ref, l_ref, light, a_ref = refs[15:]
    fields = (t_ref, k_ref, c_ref, r_ref, l_ref)
    even = lax.rem(_group(lax.axis_index("dep")), 2) == 0

    def place(left, right):
        for edge, first, seed_first in ((left, 0, SEED_HALO), (right, HALO + CORE, HALO + CORE)):
            h0[:, BASE + first : BASE + first + HALO] = edge[0:32]
            for i in range(32):
                a_ref[0, i, pl.ds(BASE + seed_first, SEED_HALO)] = edge[32 + i // 2, pl.ds(4 * (i % 2), 4)]
            light[:, BASE + first : BASE + first + HALO] = edge[48:52]

    @pl.when(even)
    def _():
        place(outer, inner)

    @pl.when(jnp.logical_not(even))
    def _():
        place(inner, outer)

    tiles = _Tiles((0, HALO + CORE), HALO, True)
    for rf in range(4):
        _properties(0, rf, tiles, [tiles.load(h0, 8 * rf + g) for g in range(8)], *fields)
    for n, source, target in ((0, h0, h1), (1, h1, h2), (2, h2, None)):
        _ghost(lambda i, c, n=n: t_ref.at[n, i, pl.ds(BASE + c, 1)])
        tiles = _Tiles((n + 1, HALO + CORE - 1 - n), HALO, True)

        def then(rf, new, n=n, target=target, tiles=tiles):
            if target is not None:
                for g in range(8):
                    tiles.store(new[g], target, 8 * rf + g)
            _properties(n + 1, rf, tiles, new, *fields)

        _advance(n, tiles, source, t_ref, k_ref, l_ref, light, then)
    for m in range(4):
        _ghost(lambda i, c, m=m: a_ref.at[m, i, pl.ds(BASE + c, 1)])
        tiles = _Tiles((SEED_HALO + m, HALO + CORE - SEED_HALO - m), HALO, True)

        def put(j, value, m=m, tiles=tiles):
            tiles.store(value, a_ref, m + 1, j)

        _retreat(3 - m, tiles, a_ref.at[m], *fields, light, put)
    core = pl.ds(BASE + HALO, CORE)
    rows = []
    sums = []
    for rf in range(4):
        value = jnp.zeros((CORE, 128), F32)
        for n in range(4):
            for g in range(8):
                lost = l_ref[n, 9 * rf + g, core] - l_ref[n, 9 * rf + g + 1, core]
                value = value + a_ref[3 - n, 8 * rf + g, core] * lost
        sums.append(value * DT)
    for z in range(NZONE):
        picked = [jnp.where(zid[rf] == float(z), sums[rf], 0.0) for rf in range(4)]
        rows.append(jnp.sum((picked[0] + picked[1]) + (picked[2] + picked[3]), axis=0, keepdims=True))
    spread = jnp.concatenate(rows + [jnp.zeros((128 - NZONE, 128), F32)], axis=0)
    zpart[...] = jnp.sum(spread.T, axis=0, keepdims=True)
    masks = [jnp.broadcast_to(m[0:1], (CORE, 128)) for m in _source_masks()]
    for g in range(8):
        turned = [a_ref[4, g, core]] + [pltpu.roll(a_ref[4, 8 * rf + g, core], 32 * rf, 1) for rf in (1, 2, 3)]
        for k, out in enumerate(outs):
            out[g] = _pick(masks, k, turned)


def unpack(own, r1, r2, r3, parts, out, total, buf):
    d = lax.axis_index("dep")
    for k, block in enumerate((own, r1, r2, r3)):
        buf[:, _columns(lax.rem(d + 4 - k, 4))] = block[...]
    for g in range(8):
        plain = buf[g].T
        for p in range(4):
            rf = lax.rem(p + 4 - d, 4)
            for sub in range(4):
                out[8 * sub + g, pl.ds(rf, 8, stride=4)] = plain[32 * p + 8 * sub : 32 * p + 8 * sub + 8]
    total[...] = jnp.sum(parts[...], axis=(0, 1))[:NZONE]


def _around(x, k):
    return lax.ppermute(x, "dep", [(s, (s + k) % 4) for s in range(4)])


def _place(y, z, core, x):
    return ((y * 4 + z) * 2 + core) * 4 + x


def _meet(v, partner):
    pairs = []
    for y in range(4):
        for z in range(4):
            for core in range(2):
                for x in range(4):
                    pairs.append((_place(y, z, core, x), _place(*partner(y, z, core, x))))
    return v + lax.ppermute(v, ("lat", "dep"), pairs)


def _shape(*dims):
    return jax.ShapeDtypeStruct(dims, F32)


def _call(kernel, inputs, outs, scratch=(), aliases=None, cost=None):
    return pl.pallas_call(
        kernel,
        out_shape=tuple(outs),
        in_specs=[_full()] * len(inputs),
        out_specs=(_full(),) * len(outs),
        scratch_shapes=list(scratch),
        input_output_aliases=aliases or {},
        cost_estimate=cost,
        compiler_params=_params(),
        name=kernel.__name__,
    )(*inputs)


def _call_hbm(kernel, inputs, outs, scratch):
    return pl.pallas_call(
        kernel,
        out_shape=tuple(outs),
        in_specs=[pl.BlockSpec(memory_space=pltpu.HBM)] * len(inputs),
        out_specs=(_full(),) * len(outs),
        scratch_shapes=list(scratch),
        compiler_params=_params(),
        name=kernel.__name__,
    )(*[pltpu.with_memory_space_constraint(x, pltpu.HBM) for x in inputs])


def _swap(x, axes, places, first):
    return lax.ppermute(
        x, axes, [pair for a, b in list(zip(places, places[1:], strict=False))[first::2] for pair in ((a, b), (b, a))]
    )


def per_device(h, zones, fluence, seed):
    piece = _shape(8, CORE, 128)
    h0, h1, h2, h3 = _call_hbm(
        pack_state, (h,), (piece,) * 4, (_vmem(32, 32, 128), _vmem(8, 128, 128), pltpu.SemaphoreType.DMA)
    )
    h2, h1, h3 = _around(h2, 2), _around(h1, 1), _around(h3, 3)
    surface = _vmem(4, HIGH, 128)
    s0, s1, s2, s3, light, zid = _call_hbm(
        pack_rest,
        (fluence, zones, seed),
        (piece,) * 4 + (surface, _shape(4, CORE, 128)),
        (
            _vmem(32, 32, 128),
            pltpu.VMEM((32, 128), jnp.int32),
            _vmem(2, 32, 128),
            _vmem(8, 128, 128),
            _vmem(2, 128, 128),
            pltpu.SMEM((NZONE,), F32),
            pltpu.SemaphoreType.DMA((3,)),
        ),
    )
    s2, s1, s3 = _around(s2, 2), _around(s1, 1), _around(s3, 3)
    one, four, five = _vmem(32, HIGH, 128), _vmem(4, 32, HIGH, 128), _vmem(5, 32, HIGH, 128)
    fields = (one, one, four, four, four, four, _vmem(4, 36, HIGH, 128))
    (state,) = _call(gather_state, (h0, h1, h3, h2), (one,))
    states = _call(forward_core, (state, light), fields)
    edge = _shape(52, HALO, 128)
    s0, light, *states = lax.optimization_barrier((s0, light, *states))
    a, to_inner, to_outer = _call(
        gather_seed, (s0, s1, s3, s2, state, light), (five, edge, edge), (_vmem(2, 52, HALO, 128),)
    )
    axes = ("lat", "dep")
    line = [4 * l + (c if l % 2 == 0 else 3 - c) for l in range(32) for c in range(4)]
    outer, inner = _swap(to_outer, axes, line, 1), _swap(to_inner, axes, line, 0)
    (a,) = _call(backward_core, (a, *states[2:], light), (five,), (), {0: 0})
    zpart, o0, o1, o2, o3 = _call(
        sides,
        (inner, outer, zid, state, *states, light, a),
        (_shape(1, 128),) + (piece,) * 4 + (one,) + fields + (surface, five),
        (),
        {3 + i: 5 + i for i in range(10)},
    )[:5]
    o2, o1, o3 = _around(o2, 2), _around(o1, 1), _around(o3, 3)
    parts = lax.all_to_all(jnp.broadcast_to(zpart[None], (128, 1, 128)), ("dep", "lat"), 0, 0)
    out, total = _call(unpack, (o0, o1, o2, o3, parts), (_shape(32, 32, 128), _shape(NZONE)), (_vmem(8, 128, 128),))
    return out, total


def solution(mesh):
    in_specs = (P("dep", None, "lat"), P(None, "lat"), P(), P("dep", None, "lat"))
    out_specs = (P("dep", None, "lat"), P())
    return jax.shard_map(per_device, mesh=mesh, in_specs=in_specs, out_specs=out_specs, check_vma=False)
```

```python
import math

import jax
import jax.numpy as jnp
from jax import lax
from jax.experimental import pallas as pl
from jax.experimental.pallas import tpu as pltpu
from jax.sharding import PartitionSpec as P


NZONE = 16
CORE = 32
HALO = 8
WIDE = CORE + 2 * HALO
SEED_HALO = 4
SEED_WIDE = CORE + 2 * SEED_HALO
BASE = 8
HIGH = WIDE + 2 * BASE
DT = 0.1
ABSORB_SOLID = 0.004
ABSORB_RISE = 0.026
LOG2E = math.log2(math.e)
EM10 = math.exp(-10.0)
F32 = jnp.float32


def _params():
    return pltpu.CompilerParams(vmem_limit_bytes=16 * 1024 * 1024)


def _group(d):
    return jnp.where(lax.rem(lax.axis_index("lat"), 2) == 0, d, 3 - d)


def _columns(d):
    return pl.ds(pl.multiple_of(_group(d) * CORE, CORE), CORE)


def _vmem(*shape):
    return pltpu.VMEM(shape, F32)


def _full():
    return pl.BlockSpec(memory_space=pltpu.VMEM)


def _lanes(rows=8):
    return lax.broadcasted_iota(jnp.int32, (rows, 128), 1)


def _packed(ref, g, d):
    tiles = []
    for p in range(4):
        rf = lax.rem(p + 4 - d, 4)
        tiles += [ref[8 * sub + g, pl.ds(rf, 8, stride=4)] for sub in range(4)]
    return jnp.concatenate(tiles, axis=0).T


def _surface(ref, rf):
    return jnp.concatenate([ref[pl.ds(rf, 8, stride=4)]] * 16, axis=0).T


def pack_state(h_in, h0, h1, h2, h3, h, buf, sem):
    d = lax.axis_index("dep")
    copy = pltpu.make_async_copy(h_in, h, sem)
    copy.start()
    copy.wait()
    for g in range(8):
        buf[g] = _packed(h, g, d)
    for k, out in enumerate((h0, h1, h2, h3)):
        out[...] = buf[:, _columns(lax.rem(d + k, 4))]


def pack_rest(fluence_in, zones_in, a_in, s0, s1, s2, s3, light, zid, a, zones, flat, buf, zbuf, fluence, sems):
    d = lax.axis_index("dep")
    copies = [
        pltpu.make_async_copy(source, target, sems.at[k])
        for k, (source, target) in enumerate(((fluence_in, fluence), (zones_in, zones), (a_in, a)))
    ]
    for copy in copies:
        copy.start()
    copies[0].wait()
    copies[1].wait()
    ids = zones[...]
    intensity = jnp.zeros(ids.shape, F32)
    for k in range(NZONE):
        intensity = jnp.where(ids == k, fluence[k] * DT, intensity)
    flat[0] = intensity
    flat[1] = ids.astype(F32)
    blank = jnp.zeros((BASE + HALO, 128), F32)
    for rf in range(4):
        zbuf[0] = _surface(flat.at[0], rf)
        light[rf, 0 : BASE + HALO] = blank
        light[rf, BASE + HALO : BASE + HALO + CORE] = zbuf[0, _columns(d)]
        light[rf, BASE + HALO + CORE :] = blank
        zbuf[1] = _surface(flat.at[1], rf)
        zid[rf] = zbuf[1, _columns(d)]
    copies[2].wait()
    for g in range(8):
        buf[g] = _packed(a, g, d)
    for k, out in enumerate((s0, s1, s2, s3)):
        out[...] = buf[:, _columns(lax.rem(d + k, 4))]


def _source_masks():
    part = lax.rem(_lanes(8) // 32 + 4 - lax.axis_index("dep"), 4)
    return [part == j for j in range(4)]


def _pick(masks, shift, values):
    return jnp.where(
        masks[shift % 4],
        values[0],
        jnp.where(masks[(shift + 1) % 4], values[1], jnp.where(masks[(shift + 2) % 4], values[2], values[3])),
    )


def _gather(blocks, field, first, count):
    masks = [jnp.broadcast_to(m[0:1], (count, 128)) for m in _source_masks()]
    for g in range(8):
        own, r1, r2, r3 = [block[g] for block in blocks]
        for rf in range(4):
            mixed = _pick(masks, rf, (own, r3, r2, r1))
            field[8 * rf + g, pl.ds(BASE + first, count)] = mixed if rf == 0 else pltpu.roll(mixed, 128 - 32 * rf, 1)


class _Tiles:
    def __init__(self, starts, count, exact):
        self.starts, self.count, self.exact = starts, count, exact
        self.rows = count * len(starts)

    def load(self, ref, *lead, shift=0):
        parts = [ref[(*lead, pl.ds(BASE + start + shift, self.count))] for start in self.starts]
        return parts[0] if len(parts) == 1 else jnp.concatenate(parts, axis=0)

    def store(self, value, ref, *lead):
        for k, start in enumerate(self.starts):
            ref[(*lead, pl.ds(BASE + start, self.count))] = value[k * self.count : (k + 1) * self.count]


def _inclusive(total, lane, reverse):
    a = lax.broadcasted_iota(jnp.int32, (128, 128), 0)
    b = lax.broadcasted_iota(jnp.int32, (128, 128), 1)
    same = lax.rem(a, 8) == lax.rem(b, 8)
    tri = jnp.where(jnp.logical_and(same, a >= b if reverse else a <= b), 1.0, 0.0).astype(jnp.bfloat16)
    high = total.astype(jnp.bfloat16)
    low = (total - high.astype(F32)).astype(jnp.bfloat16)
    return jnp.dot(jnp.concatenate([high, low], axis=1), jnp.concatenate([tri, tri], axis=0), preferred_element_type=F32)


def _properties(n, rf, tiles, states, t_ref, k_ref, c_ref, r_ref, l_ref):
    lane = _lanes(tiles.rows)
    run = jnp.zeros((tiles.rows, 128), F32)
    runs = []
    for g in range(8):
        i = 8 * rf + g
        h = states[g]
        e = jnp.exp2(h * (10.0 * LOG2E) - 10.0 * LOG2E)
        u = 1.0 + e
        v = 1.0 + EM10 * e
        inv = pl.reciprocal(u * v)
        ramp = 0.1 * jnp.log(u * (u * inv))
        t = h - ramp
        m = pl.reciprocal(1.0 + t * t)
        tiles.store(t, t_ref, n, i)
        tiles.store(0.03 + 0.04 * m, k_ref, n, i)
        tiles.store((-0.08 * t) * (m * m), c_ref, n, i)
        tiles.store(e * ((1.0 - EM10) * inv), r_ref, n, i)
        runs.append(run)
        run = run + (ABSORB_SOLID * LOG2E + (ABSORB_RISE * LOG2E) * ramp)
    above = _inclusive(run, lane, False) - run
    for g in range(8):
        tiles.store(jnp.exp2(-(above + runs[g])), l_ref, n, 9 * rf + g)
    tiles.store(jnp.exp2(-(above + run)), l_ref, n, 9 * rf + 8)


def _advance(n, tiles, h_ref, t_ref, k_ref, l_ref, light, then):
    lane = _lanes(tiles.rows)
    inside = lax.rem(lane, 8) < 7
    above_bottom = lane < 120

    def across(g):
        t3, k3 = tiles.load(t_ref, n, 24 + g), tiles.load(k_ref, n, 24 + g)
        t0, k0 = pltpu.roll(tiles.load(t_ref, n, g), 127, 1), pltpu.roll(tiles.load(k_ref, n, g), 127, 1)
        return jnp.where(inside, (k3 + k0) * (t0 - t3), 0.0)

    last = [across(g) for g in range(8)]
    before = [pltpu.roll(f, 1, 1) for f in last]
    for rf in range(4):
        i0 = 8 * rf
        t = [tiles.load(t_ref, n, i0 + g) for g in range(8)]
        k = [tiles.load(k_ref, n, i0 + g) for g in range(8)]
        end = jnp.where(above_bottom, (k[7] + pltpu.roll(k[0], 120, 1)) * (pltpu.roll(t[0], 120, 1) - t[7]), 0.0)
        flux_before = pltpu.roll(end, 8, 1)
        new = []
        for g in range(8):
            i = i0 + g
            if g < 7:
                flux = (k[g] + k[g + 1]) * (t[g + 1] - t[g])
            else:
                flux = jnp.where(above_bottom, end, -0.05 * t[7])
            if rf < 3:
                side = (k[g] + tiles.load(k_ref, n, i + 8)) * (tiles.load(t_ref, n, i + 8) - t[g])
            else:
                side = last[g]
            change = (flux - flux_before) + (side - before[g])
            col = (k[g] + tiles.load(k_ref, n, i, shift=1)) * (tiles.load(t_ref, n, i, shift=1) - t[g])
            if tiles.exact:
                col_before = (tiles.load(k_ref, n, i, shift=-1) + k[g]) * (t[g] - tiles.load(t_ref, n, i, shift=-1))
            else:
                col_before = pltpu.roll(col, 1, 0)
            change = change + (col - col_before)
            source = tiles.load(light, rf) * (tiles.load(l_ref, n, 9 * rf + g) - tiles.load(l_ref, n, 9 * rf + g + 1))
            new.append(tiles.load(h_ref, i) + (change + source))
            flux_before, before[g] = flux, side
        then(rf, new)


def _ghost(ref_rows):
    lat, group = lax.axis_index("lat"), _group(lax.axis_index("dep"))

    @pl.when(jnp.logical_and(lat == 0, group == 0))
    def _():
        for i in range(32):
            ref_rows(i, HALO - 1)[...] = ref_rows(i, HALO)[...]

    @pl.when(jnp.logical_and(lat == 31, group == 3))
    def _():
        for i in range(32):
            ref_rows(i, HALO + CORE)[...] = ref_rows(i, HALO + CORE - 1)[...]


def gather_state(own, r1, r3, r2, h0):
    _gather((own, r1, r2, r3), h0, HALO, CORE)


def gather_seed(own, r1, r3, r2, h0, light, a_ref, to_inner, to_outer, edges):
    _gather((own, r1, r2, r3), a_ref.at[0], HALO, CORE)
    for side, first, seed_first in ((0, HALO, HALO), (1, CORE, HALO + CORE - SEED_HALO)):
        edges[side, 0:32] = h0[:, BASE + first : BASE + first + HALO]
        for i in range(32):
            edges[side, 32 + i // 2, pl.ds(4 * (i % 2), 4)] = a_ref[0, i, pl.ds(BASE + seed_first, SEED_HALO)]
        edges[side, 48:52] = light[:, BASE + first : BASE + first + HALO]
    odd = lax.rem(_group(lax.axis_index("dep")), 2)
    to_inner[...] = edges[1 - odd]
    to_outer[...] = edges[odd]


def forward_core(h0, light, h1, h2, t_ref, k_ref, c_ref, r_ref, l_ref):
    fields = (t_ref, k_ref, c_ref, r_ref, l_ref)
    tiles = _Tiles((HALO,), CORE, False)
    for rf in range(4):
        _properties(0, rf, tiles, [tiles.load(h0, 8 * rf + g) for g in range(8)], *fields)
    for n, source, target in ((0, h0, h1), (1, h1, h2), (2, h2, None)):

        def then(rf, new, n=n, target=target):
            if target is not None:
                for g in range(8):
                    tiles.store(new[g], target, 8 * rf + g)
            _properties(n + 1, rf, tiles, new, *fields)

        _advance(n, tiles, source, t_ref, k_ref, l_ref, light, then)


def _retreat(n, tiles, a_ref, t_ref, k_ref, c_ref, r_ref, l_ref, light, put):
    lane = _lanes(tiles.rows)
    inside = lax.rem(lane, 8) < 7
    above_bottom = lane < 120

    def across(g):
        a3, t3, k3 = tiles.load(a_ref, 24 + g), tiles.load(t_ref, n, 24 + g), tiles.load(k_ref, n, 24 + g)
        a0, t0, k0 = [pltpu.roll(x, 127, 1) for x in (tiles.load(a_ref, g), tiles.load(t_ref, n, g), tiles.load(k_ref, n, g))]
        jump = jnp.where(inside, a3 - a0, 0.0)
        return jump * (k3 + k0), jump * (t0 - t3)

    last = [across(g) for g in range(8)]
    before = [(pltpu.roll(push, 1, 1), pltpu.roll(share, 1, 1)) for push, share in last]
    for rf in range(4):
        i0 = 8 * rf
        a = [tiles.load(a_ref, i0 + g) for g in range(8)]
        t = [tiles.load(t_ref, n, i0 + g) for g in range(8)]
        k = [tiles.load(k_ref, n, i0 + g) for g in range(8)]
        run = jnp.zeros((tiles.rows, 128), F32)
        runs = [None] * 8
        for g in reversed(range(8)):
            runs[g] = run
            run = run + a[g] * (tiles.load(l_ref, n, 9 * rf + g) - tiles.load(l_ref, n, 9 * rf + g + 1))
        below = _inclusive(run, lane, True) - run
        gain = ABSORB_RISE * tiles.load(light, rf)
        jump = jnp.where(above_bottom, a[7] - pltpu.roll(a[0], 120, 1), 0.0)
        push_end = jump * (k[7] + pltpu.roll(k[0], 120, 1))
        share_end = jump * (pltpu.roll(t[0], 120, 1) - t[7])
        push_before, share_before = pltpu.roll(push_end, 8, 1), pltpu.roll(share_end, 8, 1)
        for g in range(8):
            i = i0 + g
            if g < 7:
                jump = a[g] - a[g + 1]
                push, share = jump * (k[g] + k[g + 1]), jump * (t[g + 1] - t[g])
            else:
                push, share = jnp.where(above_bottom, push_end, 0.05 * a[7]), share_end
            if rf < 3:
                jump = a[g] - tiles.load(a_ref, i + 8)
                push_r, share_r = jump * (k[g] + tiles.load(k_ref, n, i + 8)), jump * (tiles.load(t_ref, n, i + 8) - t[g])
            else:
                push_r, share_r = last[g]
            grad_t = (push_before - push) + (before[g][0] - push_r)
            grad_k = (share_before + share) + (before[g][1] + share_r)
            jump = a[g] - tiles.load(a_ref, i, shift=1)
            push_c, share_c = jump * (k[g] + tiles.load(k_ref, n, i, shift=1)), jump * (tiles.load(t_ref, n, i, shift=1) - t[g])
            if tiles.exact:
                jump = tiles.load(a_ref, i, shift=-1) - a[g]
                push_d, share_d = jump * (tiles.load(k_ref, n, i, shift=-1) + k[g]), jump * (t[g] - tiles.load(t_ref, n, i, shift=-1))
            else:
                push_d, share_d = pltpu.roll(push_c, 1, 0), pltpu.roll(share_c, 1, 0)
            grad_t = grad_t + (push_d - push_c)
            grad_k = grad_k + (share_d + share_c)
            heat = grad_t + tiles.load(c_ref, n, i) * grad_k
            absorbed = gain * (a[g] * tiles.load(l_ref, n, 9 * rf + g + 1) - (below + runs[g]))
            put(i, a[g] + (heat + tiles.load(r_ref, n, i) * (absorbed - heat)))
            push_before, share_before, before[g] = push, share, (push_r, share_r)


def backward_core(a_in, t_ref, k_ref, c_ref, r_ref, l_ref, light, a_ref):
    tiles = _Tiles((HALO,), CORE, False)

    def step(i, carry):
        def put(j, value):
            tiles.store(value, a_ref, i + 1, j)

        _retreat(3 - i, tiles, a_ref.at[i], t_ref, k_ref, c_ref, r_ref, l_ref, light, put)
        return carry

    lax.fori_loop(0, 4, step, 0)


def sides(inner, outer, zid, *refs):
    zpart, *outs = refs[10:15]
    h0, h1, h2, t_ref, k_ref, c_ref, r_ref, l_ref, light, a_ref = refs[15:]
    fields = (t_ref, k_ref, c_ref, r_ref, l_ref)
    even = lax.rem(_group(lax.axis_index("dep")), 2) == 0

    def place(left, right):
        for edge, first, seed_first in ((left, 0, SEED_HALO), (right, HALO + CORE, HALO + CORE)):
            h0[:, BASE + first : BASE + first + HALO] = edge[0:32]
            for i in range(32):
                a_ref[0, i, pl.ds(BASE + seed_first, SEED_HALO)] = edge[32 + i // 2, pl.ds(4 * (i % 2), 4)]
            light[:, BASE + first : BASE + first + HALO] = edge[48:52]

    @pl.when(even)
    def _():
        place(outer, inner)

    @pl.when(jnp.logical_not(even))
    def _():
        place(inner, outer)

    tiles = _Tiles((0, HALO + CORE), HALO, True)
    for rf in range(4):
        _properties(0, rf, tiles, [tiles.load(h0, 8 * rf + g) for g in range(8)], *fields)
    for n, source, target in ((0, h0, h1), (1, h1, h2), (2, h2, None)):
        _ghost(lambda i, c, n=n: t_ref.at[n, i, pl.ds(BASE + c, 1)])
        tiles = _Tiles((n + 1, HALO + CORE - 1 - n), HALO, True)

        def then(rf, new, n=n, target=target, tiles=tiles):
            if target is not None:
                for g in range(8):
                    tiles.store(new[g], target, 8 * rf + g)
            _properties(n + 1, rf, tiles, new, *fields)

        _advance(n, tiles, source, t_ref, k_ref, l_ref, light, then)
    for m in range(4):
        _ghost(lambda i, c, m=m: a_ref.at[m, i, pl.ds(BASE + c, 1)])
        tiles = _Tiles((SEED_HALO + m, HALO + CORE - SEED_HALO - m), HALO, True)

        def put(j, value, m=m, tiles=tiles):
            tiles.store(value, a_ref, m + 1, j)

        _retreat(3 - m, tiles, a_ref.at[m], *fields, light, put)
    core = pl.ds(BASE + HALO, CORE)
    rows = []
    sums = []
    for rf in range(4):
        value = jnp.zeros((CORE, 128), F32)
        for n in range(4):
            for g in range(8):
                lost = l_ref[n, 9 * rf + g, core] - l_ref[n, 9 * rf + g + 1, core]
                value = value + a_ref[3 - n, 8 * rf + g, core] * lost
        sums.append(value * DT)
    for z in range(NZONE):
        picked = [jnp.where(zid[rf] == float(z), sums[rf], 0.0) for rf in range(4)]
        rows.append(jnp.sum((picked[0] + picked[1]) + (picked[2] + picked[3]), axis=0, keepdims=True))
    spread = jnp.concatenate(rows + [jnp.zeros((128 - NZONE, 128), F32)], axis=0)
    zpart[...] = jnp.sum(spread.T, axis=0, keepdims=True)
    masks = [jnp.broadcast_to(m[0:1], (CORE, 128)) for m in _source_masks()]
    for g in range(8):
        turned = [a_ref[4, g, core]] + [pltpu.roll(a_ref[4, 8 * rf + g, core], 32 * rf, 1) for rf in (1, 2, 3)]
        for k, out in enumerate(outs):
            out[g] = _pick(masks, k, turned)


def unpack(own, r1, r2, r3, parts, out, total, buf):
    d = lax.axis_index("dep")
    for k, block in enumerate((own, r1, r2, r3)):
        buf[:, _columns(lax.rem(d + 4 - k, 4))] = block[...]
    for g in range(8):
        plain = buf[g].T
        for p in range(4):
            rf = lax.rem(p + 4 - d, 4)
            for sub in range(4):
                out[8 * sub + g, pl.ds(rf, 8, stride=4)] = plain[32 * p + 8 * sub : 32 * p + 8 * sub + 8]
    total[...] = jnp.sum(parts[...], axis=(0, 1))[:NZONE]


def _around(x, k):
    return lax.ppermute(x, "dep", [(s, (s + k) % 4) for s in range(4)])


def _place(y, z, core, x):
    return ((y * 4 + z) * 2 + core) * 4 + x


def _meet(v, partner):
    pairs = []
    for y in range(4):
        for z in range(4):
            for core in range(2):
                for x in range(4):
                    pairs.append((_place(y, z, core, x), _place(*partner(y, z, core, x))))
    return v + lax.ppermute(v, ("lat", "dep"), pairs)


def _shape(*dims):
    return jax.ShapeDtypeStruct(dims, F32)


def _call(kernel, inputs, outs, scratch=(), aliases=None, cost=None):
    return pl.pallas_call(
        kernel,
        out_shape=tuple(outs),
        in_specs=[_full()] * len(inputs),
        out_specs=(_full(),) * len(outs),
        scratch_shapes=list(scratch),
        input_output_aliases=aliases or {},
        cost_estimate=cost,
        compiler_params=_params(),
        name=kernel.__name__,
    )(*inputs)


def _call_hbm(kernel, inputs, outs, scratch):
    return pl.pallas_call(
        kernel,
        out_shape=tuple(outs),
        in_specs=[pl.BlockSpec(memory_space=pltpu.HBM)] * len(inputs),
        out_specs=(_full(),) * len(outs),
        scratch_shapes=list(scratch),
        compiler_params=_params(),
        name=kernel.__name__,
    )(*[pltpu.with_memory_space_constraint(x, pltpu.HBM) for x in inputs])


def _swap(x, axes, places, first):
    return lax.ppermute(
        x, axes, [pair for a, b in list(zip(places, places[1:], strict=False))[first::2] for pair in ((a, b), (b, a))]
    )


def per_device(h, zones, fluence, seed):
    piece = _shape(8, CORE, 128)
    h0, h1, h2, h3 = _call_hbm(
        pack_state, (h,), (piece,) * 4, (_vmem(32, 32, 128), _vmem(8, 128, 128), pltpu.SemaphoreType.DMA)
    )
    h2, h1, h3 = _around(h2, 2), _around(h1, 1), _around(h3, 3)
    surface = _vmem(4, HIGH, 128)
    s0, s1, s2, s3, light, zid = _call_hbm(
        pack_rest,
        (fluence, zones, seed),
        (piece,) * 4 + (surface, _shape(4, CORE, 128)),
        (
            _vmem(32, 32, 128),
            pltpu.VMEM((32, 128), jnp.int32),
            _vmem(2, 32, 128),
            _vmem(8, 128, 128),
            _vmem(2, 128, 128),
            pltpu.SMEM((NZONE,), F32),
            pltpu.SemaphoreType.DMA((3,)),
        ),
    )
    s2, s1, s3 = _around(s2, 2), _around(s1, 1), _around(s3, 3)
    one, four, five = _vmem(32, HIGH, 128), _vmem(4, 32, HIGH, 128), _vmem(5, 32, HIGH, 128)
    fields = (one, one, four, four, four, four, _vmem(4, 36, HIGH, 128))
    (state,) = _call(gather_state, (h0, h1, h3, h2), (one,))
    states = _call(forward_core, (state, light), fields)
    edge = _shape(52, HALO, 128)
    s0, light, *states = lax.optimization_barrier((s0, light, *states))
    a, to_inner, to_outer = _call(
        gather_seed, (s0, s1, s3, s2, state, light), (five, edge, edge), (_vmem(2, 52, HALO, 128),)
    )
    axes = ("lat", "dep")
    line = [4 * l + (c if l % 2 == 0 else 3 - c) for l in range(32) for c in range(4)]
    outer, inner = _swap(to_outer, axes, line, 1), _swap(to_inner, axes, line, 0)
    (a,) = _call(backward_core, (a, *states[2:], light), (five,), (), {0: 0})
    zpart, o0, o1, o2, o3 = _call(
        sides,
        (inner, outer, zid, state, *states, light, a),
        (_shape(1, 128),) + (piece,) * 4 + (one,) + fields + (surface, five),
        (),
        {3 + i: 5 + i for i in range(10)},
    )[:5]
    o2, o1, o3 = _around(o2, 2), _around(o1, 1), _around(o3, 3)
    parts = lax.all_to_all(jnp.broadcast_to(zpart[None], (128, 1, 128)), ("dep", "lat"), 0, 0)
    out, total = _call(unpack, (o0, o1, o2, o3, parts), (_shape(32, 32, 128), _shape(NZONE)), (_vmem(8, 128, 128),))
    return out, total


def solution(mesh):
    in_specs = (P("dep", None, "lat"), P(None, "lat"), P(), P("dep", None, "lat"))
    out_specs = (P("dep", None, "lat"), P())
    return jax.shard_map(per_device, mesh=mesh, in_specs=in_specs, out_specs=out_specs, check_vma=False)
```
